32 devices in a mesh: seq: 8 (over z, y), tp: 4 (over x, core).
Axes of the slice: x: 2, y: 2, z: 4, core: 2. Of those that a mesh axis runs over, the one named last changes fastest.
Arguments:
- short_hidden: bfloat16 [128, 1280], P('seq', 'tp'), may hold values from -6 to 6
- long_hidden: bfloat16 [4, 1280], P(None, 'tp'), may hold values from -6 to 6
- short_len: int32 [128], replicated, may hold values from 1 to 127
- short_slot: int32 [128], replicated, may hold values from 0 to 255, as said below
- w_query: bfloat16 [1280, 1280], P(None, 'tp'), may hold values from -0.15625 to 0.15625
- w_key: bfloat16 [1280, 1280], P(None, 'tp'), may hold values from -0.15625 to 0.15625
- w_value: bfloat16 [1280, 1280], P(None, 'tp'), may hold values from -0.15625 to 0.15625
- w_out: bfloat16 [1280, 1280], P('tp'), may hold values from -0.15625 to 0.15625
- qk_gain: float32 [1280], P('tp'), may hold values from 0.7 to 2
- step_rate: float32 [1280], replicated, may hold values from 0.1 to 0.6
- short_keys: bfloat16 [256, 128, 1280], P('seq', None, 'tp'), may hold values from -0.19921875 to 0.19921875
- short_values: bfloat16 [256, 128, 1280], P('seq', None, 'tp'), may hold values from -6 to 6
- long_keys: bfloat16 [4, 4096, 1280], P(None, 'seq', 'tp'), may hold values from -0.19921875 to 0.19921875
- long_values: bfloat16 [4, 4096, 1280], P(None, 'seq', 'tp'), may hold values from -6 to 6
Outputs:
- short_out: bfloat16 [128, 1280], P('seq', 'tp')
- long_out: bfloat16 [4, 1280], P(None, 'tp')
The draws below stay inside these ranges and needn't reach their ends.
Inputs may be any that keep to these rules, and one draw needn't show every extreme that they name: `short_slot`: all slot numbers are distinct; slot s is row s of short_keys and short_values, so it lies on index s // 32 of seq. In every draw some index of seq has all 32 of its slots taken.
All inputs are finite; a program needn't handle non-finite values.
Results may differ from the reference program's by a relative error of at most 0.01.
Values may be sent and summed in bfloat16 or wider, within the bound.
No kernel may reach another device: no remote copies, remote signals or barrier semaphores. Data moves between devices by JAX's collectives and lax.ppermute only.
A program may use at most 64 MiB of HBM per device.

```python
import math
import jax
import jax.numpy as jnp
from jax import lax

D = 1280
HEADS = 20
HEAD = 64
CAP = 128
LONG = 4
SLOT_DEV = 32
SHORT = 128
SLOTS = 256
LONG_LEN = 4096


def draw_short_slot(key, part):
    base = jax.random.fold_in(key, 11)
    key_hot, key_bias, key_score, key_order = jax.random.split(base, 4)
    shards = SLOTS // SLOT_DEV
    slot_ids = jnp.arange(SLOTS, dtype=jnp.int32)
    shard_of = slot_ids // SLOT_DEV
    hot = jax.random.randint(key_hot, (), 0, shards, dtype=jnp.int32)
    bias = jax.random.randint(key_bias, (shards,), 0, 4, dtype=jnp.int32)
    score = jax.random.randint(key_score, (SLOTS,), 0, 1024, dtype=jnp.int32)
    score = score + bias[shard_of] * 1024
    score = jnp.where(shard_of == hot, score - 8192, score)
    ends = (slot_ids == 0) | (slot_ids == SLOTS - 1)
    score = jnp.where(ends, score - 16384, score) + 16384
    order = jnp.argsort(score * SLOTS + slot_ids, stable=True)
    chosen = order[:SHORT].astype(jnp.int32)
    mixing = jax.random.permutation(key_order, SHORT)
    return chosen[mixing].astype(jnp.int32)


def touch_ends(values, own_key, smallest, top_value):
    shape = values.shape
    spot = [jax.random.randint(jax.random.fold_in(own_key, axis), (), 0, shape[axis]) for axis in range(len(shape))]
    values = values.at[tuple(spot)].set(smallest)
    longest = shape.index(max(shape))
    spot[longest] = (spot[longest] + 1) % shape[longest]
    return values.at[tuple(spot)].set(top_value)


def shard_levels(stream_key, extent, cuts, least, largest):
    def one(dim, blocks):
        steps = jax.random.uniform(jax.random.fold_in(jax.random.fold_in(stream_key, 6), dim), (blocks,), jnp.float32, least / len(cuts), largest / len(cuts))
        return jnp.repeat(jnp.exp(steps), extent[dim] // blocks).reshape((-1,) + (1,) * (len(extent) - dim - 1))

    factor_of = one(*cuts[0])
    for cut in cuts[1:]:
        factor_of = factor_of * one(*cut)
    return factor_of


def scatter_about(key, extent, width, reach, cuts=(), kind=jnp.bfloat16):
    loudness = shard_levels(key, extent, cuts, -0.22, 0.18) if cuts else 1.0
    entries = jax.random.normal(key, extent, jnp.float32) * width * loudness
    return jnp.minimum(jnp.maximum(entries, -reach), reach).astype(kind)


def setup_inputs(seed: int = 0) -> dict:
    splits = jax.random.split(jax.random.key(seed), 15)
    return {
        "short_hidden": scatter_about(splits[0], (SHORT, D), 1.0, 6.0, ((0, 8), (1, 4))),
        "long_hidden": scatter_about(splits[1], (LONG, D), 1.0, 6.0, ((1, 4),)),
        "short_len": touch_ends(jax.random.randint(splits[2], (SHORT,), 1, CAP), jax.random.fold_in(splits[2], 1), 1, CAP - 1).astype(jnp.int32),
        "short_slot": draw_short_slot(jax.random.fold_in(splits[14], 71), 0),
        "w_query": scatter_about(splits[4], (D, D), D ** -0.5, 0.15625, ((1, 4),)),
        "w_key": scatter_about(splits[5], (D, D), D ** -0.5, 0.15625, ((1, 4),)),
        "w_value": scatter_about(splits[6], (D, D), D ** -0.5, 0.15625, ((1, 4),)),
        "w_out": scatter_about(splits[7], (D, D), D ** -0.5, 0.15625, ((0, 4),)),
        "qk_gain": jnp.clip(jnp.exp(math.log(2.0) - 1.0498221 * jax.random.uniform(splits[8], (D,), jnp.float32) ** shard_levels(splits[8], (D,), ((0, 4),), -0.2, 0.2)), 0.7, 2.0),
        "step_rate": jnp.clip(jnp.exp(jax.random.uniform(splits[9], (D,), jnp.float32, math.log(0.1), math.log(0.6))), 0.1, 0.6),
        "short_keys": jnp.clip(jax.random.uniform(splits[10], (SLOTS, CAP, D), jnp.float32, -0.19921875, 0.19921875) * shard_levels(splits[10], (SLOTS, CAP, D), ((0, 8), (2, 4)), -0.4, 0.0), -0.19921875, 0.19921875).astype(jnp.bfloat16),
        "short_values": scatter_about(splits[11], (SLOTS, CAP, D), 1.0, 6.0, ((0, 8), (2, 4))),
        "long_keys": jnp.clip(jax.random.uniform(splits[12], (LONG, LONG_LEN, D), jnp.float32, -0.19921875, 0.19921875) * shard_levels(splits[12], (LONG, LONG_LEN, D), ((1, 8), (2, 4)), -0.4, 0.0), -0.19921875, 0.19921875).astype(jnp.bfloat16),
        "long_values": scatter_about(splits[13], (LONG, LONG_LEN, D), 1.0, 6.0, ((1, 8), (2, 4))),
    }


EPS = 1e-06

def head_unit(x, gain):
    count = x.shape[0]
    parts = x.reshape(count, -1, HEAD)
    parts = parts * lax.rsqrt(lax.optimization_barrier(jnp.sum(parts * parts, -1, keepdims=True)) + EPS)
    return parts.reshape(count, -1) * gain

def row_unit(x):
    return x * lax.rsqrt(lax.optimization_barrier(jnp.mean(x * x, -1, keepdims=True)) + EPS)

def widen(x):
    return lax.optimization_barrier(x.astype(jnp.bfloat16)).astype(jnp.float32)

def cache_terms(query, keys, values, live):
    positions = keys.shape[0]
    key_f = keys.astype(jnp.float32).reshape(positions, HEADS, HEAD)
    value_f = values.astype(jnp.float32).reshape(positions, HEADS, HEAD)
    scores = jnp.einsum('he,phe->hp', query, key_f) * math.sqrt(HEAD)
    weights = jnp.where(live[None, :], jnp.exp(scores), jnp.float32(0.0))
    den = lax.optimization_barrier(jnp.sum(weights, -1))
    num = jnp.einsum('hp,phe->he', widen(weights), value_f)
    return (num, den)

def reference(short_hidden, long_hidden, short_len, short_slot, w_query, w_key, w_value, w_out, qk_gain, step_rate, short_keys, short_values, long_keys, long_values):
    rows = jnp.concatenate([short_hidden, long_hidden], 0)
    count = rows.shape[0]
    q_proj = jnp.dot(rows, w_query, preferred_element_type=jnp.float32)
    k_proj = jnp.dot(rows, w_key, preferred_element_type=jnp.float32)
    v_proj = jnp.dot(rows, w_value, preferred_element_type=jnp.float32)
    query = head_unit(q_proj, qk_gain).astype(jnp.bfloat16)
    new_key = head_unit(k_proj, qk_gain).astype(jnp.bfloat16)
    new_value = v_proj.astype(jnp.bfloat16)
    query_f = query.astype(jnp.float32).reshape(count, HEADS, HEAD)
    key_f = new_key.astype(jnp.float32).reshape(count, HEADS, HEAD)
    value_f = new_value.astype(jnp.float32).reshape(count, HEADS, HEAD)

    def short_one(item):
        query_row, slot, length = item
        keys = lax.dynamic_index_in_dim(short_keys, slot.astype(jnp.int32), 0, keepdims=False)
        values = lax.dynamic_index_in_dim(short_values, slot.astype(jnp.int32), 0, keepdims=False)
        live = jnp.arange(CAP, dtype=jnp.int32) < length
        return cache_terms(query_row, keys, values, live)

    def long_one(item):
        query_row, keys, values = item
        live = jnp.ones((LONG_LEN,), dtype=bool)
        return cache_terms(query_row, keys, values, live)
    short_num, short_den = lax.map(short_one, (query_f[:SHORT], short_slot, short_len))
    long_num, long_den = lax.map(long_one, (query_f[SHORT:], long_keys, long_values))
    cache_num = jnp.concatenate([short_num, long_num], 0)
    cache_den = jnp.concatenate([short_den, long_den], 0)
    own = jnp.exp(lax.optimization_barrier(jnp.sum(query_f * key_f, -1)) * math.sqrt(HEAD))
    den = cache_den + own
    num = cache_num + widen(own)[..., None] * value_f
    attended = (num / den[..., None]).reshape(count, D).astype(jnp.bfloat16)
    proj = jnp.dot(attended, w_out, preferred_element_type=jnp.float32)
    state = rows.astype(jnp.float32)
    update = state + step_rate * (row_unit(proj) - state)
    result = row_unit(update).astype(jnp.bfloat16)
    return (result[:SHORT], result[SHORT:])
```

```python
import functools
import math

import jax
import jax.numpy as jnp
from jax import lax
from jax.experimental import pallas as pl
from jax.experimental.pallas import tpu as pltpu
from jax.sharding import PartitionSpec as P

HEAD = 64
EPS = 1e-06
SUB = 8
BF16 = jnp.bfloat16
F32 = jnp.float32
NT = (((1,), (1,)), ((), ()))


def lanes(shape):
    return lax.broadcasted_iota(jnp.int32, shape, len(shape) - 1)


def rows_of(shape):
    return lax.broadcasted_iota(jnp.int32, shape, len(shape) - 2)


def head_cols(x):
    head = lanes(x.shape) // HEAD
    return [
        jnp.sum(jnp.where(head == h, x, 0.0), -1, keepdims=True)
        for h in range(x.shape[-1] // HEAD)
    ]


def spread_cols(cols, shape):
    head = lanes(shape) // HEAD
    out = jnp.broadcast_to(cols[0], shape)
    for h in range(1, len(cols)):
        out = jnp.where(head == h, cols[h], out)
    return out


def head_unit(x, gain):
    scale = spread_cols([lax.rsqrt(c + EPS) for c in head_cols(x * x)], x.shape)
    return x * scale * gain


def project(h_ref, w_ref):
    parts, _, chunk = h_ref.shape
    total = None
    for t in range(parts):
        term = jnp.dot(
            h_ref[t], w_ref[t * chunk : (t + 1) * chunk, :], preferred_element_type=F32
        )
        total = term if total is None else total + term
    return total


def query_kernel(h_ref, w_ref, gain_ref, send_ref, query_ref):
    query = head_unit(project(h_ref, w_ref), gain_ref[...]).astype(BF16)
    query_ref[...] = query
    groups, n_short, _ = send_ref.shape
    for g in range(groups):
        send_ref[g] = query[:n_short]


def den_tile(den, width):
    high = den.astype(BF16).astype(F32)
    low = den - high
    lane, row = lanes((SUB, width)), rows_of((SUB, width))
    return jnp.where(lane == row, high, jnp.where(lane == row + SUB, low, 0.0))


def local_kernel(n_short, h_ref, wk_ref, wv_ref, gain_ref, q_ref, lk_ref, lv_ref, den_ref, num_ref, pay_ref):
    long_count, _, width = lk_ref.shape
    heads = width // HEAD
    query = q_ref[...].astype(F32)
    new_key = head_unit(project(h_ref, wk_ref), gain_ref[...]).astype(BF16).astype(F32)
    new_value = project(h_ref, wv_ref).astype(BF16).astype(F32)
    own = [jnp.exp(c * math.sqrt(HEAD)) for c in head_cols(query * new_key)]
    den_ref[...] = spread_cols(own, query.shape)
    num_ref[...] = (
        spread_cols([o.astype(BF16).astype(F32) for o in own], query.shape) * new_value
    )
    shape = (SUB, width)
    mask = (lanes(shape) // HEAD) == rows_of(shape)
    pay_ref[...] = jnp.zeros(pay_ref.shape, F32)
    for i in range(long_count):
        row = query[n_short + i : n_short + i + 1] * math.sqrt(HEAD)
        blocks = jnp.where(mask, jnp.broadcast_to(row, shape), 0.0).astype(BF16)
        scores = lax.dot_general(blocks, lk_ref[i], NT, preferred_element_type=F32)
        weights = jnp.exp(scores)
        den = jnp.sum(weights, -1, keepdims=True)
        num = jnp.dot(weights.astype(BF16), lv_ref[i], preferred_element_type=F32)
        pay_ref[i : i + 1, :width] = jnp.sum(jnp.where(mask, num, 0.0), 0, keepdims=True)
        tail = pay_ref.shape[1] - width
        pay_ref[i : i + 1, width:] = jnp.sum(
            jnp.where(rows_of((SUB, tail)) < heads, den_tile(den, tail), 0.0), 0, keepdims=True
        )


def short_kernel(pos_row_ref, pos_col_ref, len_ref, q_ref, k_ref, v_ref, long_ref, out_ref, num_ref):
    slots, capacity, width = k_ref.shape
    groups, n_short, _ = q_ref.shape
    total = groups * n_short
    heads = width // HEAD
    exp_rows = slots * SUB
    hit = pos_row_ref[...] == rows_of((exp_rows, total)) // SUB
    queries = q_ref[...].reshape(total, width)
    picked = jnp.dot(hit.astype(BF16), queries, preferred_element_type=F32)
    shape = (exp_rows, width)
    mask = (lanes(shape) // HEAD) == (rows_of(shape) % SUB)
    blocks = jnp.where(mask, picked * math.sqrt(HEAD), 0.0).astype(BF16)
    lengths = jnp.sum(jnp.where(hit, len_ref[...], 0), -1, keepdims=True)
    tail = out_ref.shape[-1] - width
    real = rows_of((SUB, tail)) < heads
    mask8 = mask[:SUB]
    for s in range(slots):
        at = slice(s * SUB, (s + 1) * SUB)
        scores = lax.dot_general(blocks[at], k_ref[s], NT, preferred_element_type=F32)
        weights = jnp.where(lanes((SUB, capacity)) < lengths[at], jnp.exp(scores), 0.0)
        den = jnp.sum(weights, -1, keepdims=True)
        num = jnp.dot(weights.astype(BF16), v_ref[s], preferred_element_type=F32)
        num_ref[at, :width] = jnp.where(mask8, num, 0.0)
        num_ref[at, width:] = jnp.where(real, den_tile(den, tail), 0.0)
    spread = (pos_col_ref[...] == lanes((total, exp_rows)) // SUB).astype(BF16)
    sent = jnp.dot(spread, num_ref[...].astype(BF16), preferred_element_type=F32).astype(BF16)
    out_ref[:, :n_short, :] = sent.reshape(groups, n_short, out_ref.shape[-1])
    extra = long_ref[...].astype(BF16)
    for g in range(groups):
        out_ref[g, n_short:, :] = extra


def combine_kernel(back_ref, den_ref, num_ref, w_ref, out_ref):
    width = num_ref.shape[-1]
    heads = width // HEAD
    total = back_ref[0].astype(F32)
    for g in range(1, back_ref.shape[0]):
        total = total + back_ref[g].astype(F32)
    dens = total[:, width:]
    cols = [dens[:, h : h + 1] + dens[:, SUB + h : SUB + h + 1] for h in range(heads)]
    den = den_ref[...] + spread_cols(cols, num_ref.shape)
    attended = ((total[:, :width] + num_ref[...]) / den).astype(BF16)
    out_ref[...] = jnp.dot(attended, w_ref[...], preferred_element_type=F32).astype(BF16)


def final_kernel(tp_ref, part_ref, h_ref, rate_ref, short_ref, long_ref):
    parts, rows, width = h_ref.shape
    n_short, n_long = short_ref.shape[0], long_ref.shape[0]
    features = parts * width
    proj = part_ref[0].astype(F32)
    for t in range(1, part_ref.shape[0]):
        proj = proj + part_ref[t].astype(F32)
    proj = proj * lax.rsqrt(jnp.sum(proj * proj, -1, keepdims=True) / features + EPS)
    mine = jnp.zeros((rows, width), F32)
    square = jnp.zeros((rows, width), F32)
    for t in range(parts):
        cut = slice(t * width, (t + 1) * width)
        state = h_ref[t].astype(F32)
        update = state + rate_ref[:, cut] * (proj[:, cut] - state)
        square = square + update * update
        mine = jnp.where(tp_ref[0] == t, update, mine)
    result = mine * lax.rsqrt(jnp.sum(square, -1, keepdims=True) / features + EPS)
    result = result.astype(BF16)
    short_ref[...] = result[:n_short]
    long_ref[...] = result[n_short : n_short + n_long]


VMEM = pl.BlockSpec(memory_space=pltpu.VMEM)
SMEM = pl.BlockSpec(memory_space=pltpu.SMEM)


def call(kernel, outs, ins, flops, moved, scratch=(), specs=None, limit=16):
    return pl.pallas_call(
        kernel,
        out_shape=outs,
        in_specs=specs or [VMEM] * len(ins),
        out_specs=jax.tree.map(lambda _: VMEM, outs),
        scratch_shapes=scratch,
        compiler_params=pltpu.CompilerParams(vmem_limit_bytes=limit * 1024 * 1024),
        cost_estimate=pl.CostEstimate(flops=flops, bytes_accessed=moved, transcendentals=0),
    )(*ins)


def on_device(
    short_hidden,
    long_hidden,
    short_len,
    short_slot,
    w_query,
    w_key,
    w_value,
    w_out,
    qk_gain,
    step_rate,
    short_keys,
    short_values,
    long_keys,
    long_values,
):
    n_short, width = short_hidden.shape
    n_long = long_hidden.shape[0]
    groups = lax.axis_size("seq")
    features = w_query.shape[0]
    slots, capacity, _ = short_keys.shape
    total = short_len.shape[0]
    pad = -(n_short + n_long) % SUB
    count = n_short + n_long + pad
    sent_width = -(-(width + 2 * SUB) // 128) * 128
    out = jax.ShapeDtypeStruct

    mine = jnp.concatenate([short_hidden, long_hidden, jnp.zeros((pad, width), BF16)], 0)
    hidden = lax.all_gather(mine, "tp", axis=0)
    gain = qk_gain.reshape(1, width)
    position = short_slot - lax.axis_index("seq") * slots
    tp_index = lax.axis_index("tp").reshape(1)

    send, query = call(
        query_kernel,
        (out((groups, n_short, width), BF16), out((count, width), BF16)),
        (hidden, w_query, gain),
        2 * count * features * width,
        2 * features * width,
    )
    queries = lax.all_to_all(send, "seq", split_axis=0, concat_axis=0, tiled=True)
    own_den, own_num, long_part = call(
        functools.partial(local_kernel, n_short),
        (out((count, width), F32), out((count, width), F32), out((count - n_short, sent_width), F32)),
        (hidden, w_key, w_value, gain, query, long_keys, long_values),
        4 * count * features * width,
        4 * features * width + 4 * long_keys.size,
    )
    sent = call(
        short_kernel,
        out((groups, count, sent_width), BF16),
        (
            position.reshape(1, total),
            position.reshape(total, 1),
            short_len.reshape(1, total),
            queries,
            short_keys,
            short_values,
            long_part,
        ),
        4 * short_keys.size * SUB,
        4 * short_keys.size,
        scratch=[pltpu.VMEM((slots * SUB, sent_width), F32)],
    )
    back = lax.all_to_all(sent, "seq", split_axis=0, concat_axis=0, tiled=True)
    partial = call(
        combine_kernel,
        out((count, features), BF16),
        (back, own_den, own_num, w_out),
        2 * count * features * width,
        2 * features * width,
    )
    partials = lax.all_gather(partial, "tp", axis=0)
    return call(
        final_kernel,
        (out((n_short, width), BF16), out((n_long, width), BF16)),
        (tp_index, partials, hidden, step_rate.reshape(1, features)),
        10 * count * features,
        10 * count * features,
        specs=[SMEM, VMEM, VMEM, VMEM],
    )


def solution(mesh):
    return jax.shard_map(
        on_device,
        mesh=mesh,
        in_specs=(
            P("seq", "tp"),
            P(None, "tp"),
            P(),
            P(),
            P(None, "tp"),
            P(None, "tp"),
            P(None, "tp"),
            P("tp", None),
            P("tp"),
            P(),
            P("seq", None, "tp"),
            P("seq", None, "tp"),
            P(None, "seq", "tp"),
            P(None, "seq", "tp"),
        ),
        out_specs=(P("seq", "tp"), P(None, "tp")),
        check_vma=False,
    )
```

```python
import functools
import math

import jax
import jax.numpy as jnp
from jax import lax
from jax.experimental import pallas as pl
from jax.experimental.pallas import tpu as pltpu
from jax.sharding import PartitionSpec as P

HEAD = 64
EPS = 1e-06
SUB = 8
BF16 = jnp.bfloat16
F32 = jnp.float32
NT = (((1,), (1,)), ((), ()))


def lanes(shape):
    return lax.broadcasted_iota(jnp.int32, shape, len(shape) - 1)


def rows_of(shape):
    return lax.broadcasted_iota(jnp.int32, shape, len(shape) - 2)


def head_cols(x):
    head = lanes(x.shape) // HEAD
    return [
        jnp.sum(jnp.where(head == h, x, 0.0), -1, keepdims=True)
        for h in range(x.shape[-1] // HEAD)
    ]


def spread_cols(cols, shape):
    head = lanes(shape) // HEAD
    out = jnp.broadcast_to(cols[0], shape)
    for h in range(1, len(cols)):
        out = jnp.where(head == h, cols[h], out)
    return out


def head_unit(x, gain):
    scale = spread_cols([lax.rsqrt(c + EPS) for c in head_cols(x * x)], x.shape)
    return x * scale * gain


def project(rows, w_ref):
    return lax.dot_general(rows, w_ref[...], NT, preferred_element_type=F32)


def query_kernel(tp_ref, *refs):
    *piece_refs, w_ref, gain_ref, send_ref, query_ref, rows_ref, order_ref = refs
    for k, piece in enumerate(piece_refs):
        order_ref[sender(tp_ref[0], k, len(piece_refs))] = piece[...].astype(F32)
    rows = jnp.concatenate([order_ref[t] for t in range(len(piece_refs))], 1).astype(BF16)
    rows_ref[...] = rows
    query = head_unit(project(rows, w_ref), gain_ref[...]).astype(BF16)
    query_ref[...] = query
    groups, n_short, _ = send_ref.shape
    for g in range(groups):
        send_ref[g] = query[:n_short]


def den_tile(den, width):
    high = den.astype(BF16).astype(F32)
    low = den - high
    lane, row = lanes((SUB, width)), rows_of((SUB, width))
    return jnp.where(lane == row, high, jnp.where(lane == row + SUB, low, 0.0))


def local_kernel(n_short, rows_ref, wk_ref, wv_ref, gain_ref, q_ref, lk_ref, lv_ref, den_ref, num_ref, pay_ref):
    long_count, width, _ = lk_ref.shape
    heads = width // HEAD
    query = q_ref[...].astype(F32)
    rows = rows_ref[...]
    new_key = head_unit(project(rows, wk_ref), gain_ref[...]).astype(BF16).astype(F32)
    new_value = project(rows, wv_ref).astype(BF16).astype(F32)
    own = [jnp.exp(c * math.sqrt(HEAD)) for c in head_cols(query * new_key)]
    den_ref[...] = spread_cols(own, query.shape)
    num_ref[...] = (
        spread_cols([o.astype(BF16).astype(F32) for o in own], query.shape) * new_value
    )
    shape = (SUB, width)
    mask = (lanes(shape) // HEAD) == rows_of(shape)
    pay_ref[...] = jnp.zeros(pay_ref.shape, F32)
    for i in range(long_count):
        row = query[n_short + i : n_short + i + 1] * math.sqrt(HEAD)
        blocks = jnp.where(mask, jnp.broadcast_to(row, shape), 0.0).astype(BF16)
        scores = jnp.dot(blocks, lk_ref[i], preferred_element_type=F32)
        weights = jnp.exp(scores)
        den = jnp.sum(weights, -1, keepdims=True)
        num = lax.dot_general(weights.astype(BF16), lv_ref[i], NT, preferred_element_type=F32)
        pay_ref[i : i + 1, :width] = jnp.sum(jnp.where(mask, num, 0.0), 0, keepdims=True)
        tail = pay_ref.shape[1] - width
        pay_ref[i : i + 1, width:] = jnp.sum(
            jnp.where(rows_of((SUB, tail)) < heads, den_tile(den, tail), 0.0), 0, keepdims=True
        )


def short_kernel(pos_row_ref, pos_col_ref, len_ref, q_ref, k_ref, v_ref, long_ref, out_ref, num_ref):
    slots, width, capacity = k_ref.shape
    groups, n_short, _ = q_ref.shape
    total = groups * n_short
    heads = width // HEAD
    exp_rows = slots * SUB
    hit = pos_row_ref[...] == rows_of((exp_rows, total)) // SUB
    queries = q_ref[...].reshape(total, width)
    picked = jnp.dot(hit.astype(BF16), queries, preferred_element_type=F32)
    shape = (exp_rows, width)
    mask = (lanes(shape) // HEAD) == (rows_of(shape) % SUB)
    blocks = jnp.where(mask, picked * math.sqrt(HEAD), 0.0).astype(BF16)
    lengths = jnp.sum(jnp.where(hit, len_ref[...], 0), -1, keepdims=True)
    tail = out_ref.shape[-1] - width
    real = rows_of((SUB, tail)) < heads
    mask8 = mask[:SUB]
    for s in range(slots):
        at = slice(s * SUB, (s + 1) * SUB)
        scores = jnp.dot(blocks[at], k_ref[s], preferred_element_type=F32)
        weights = jnp.where(lanes((SUB, capacity)) < lengths[at], jnp.exp(scores), 0.0)
        den = jnp.sum(weights, -1, keepdims=True)
        num = lax.dot_general(weights.astype(BF16), v_ref[s], NT, preferred_element_type=F32)
        num_ref[at, :width] = jnp.where(mask8, num, 0.0)
        num_ref[at, width:] = jnp.where(real, den_tile(den, tail), 0.0)
    spread = (pos_col_ref[...] == lanes((total, exp_rows)) // SUB).astype(BF16)
    sent = jnp.dot(spread, num_ref[...].astype(BF16), preferred_element_type=F32).astype(BF16)
    out_ref[:, :n_short, :] = sent.reshape(groups, n_short, out_ref.shape[-1])
    extra = long_ref[...].astype(BF16)
    for g in range(groups):
        out_ref[g, n_short:, :] = extra


def combine_kernel(back_ref, den_ref, num_ref, w_ref, out_ref):
    width = num_ref.shape[-1]
    heads = width // HEAD
    total = back_ref[0].astype(F32)
    for g in range(1, back_ref.shape[0]):
        total = total + back_ref[g].astype(F32)
    dens = total[:, width:]
    cols = [dens[:, h : h + 1] + dens[:, SUB + h : SUB + h + 1] for h in range(heads)]
    den = den_ref[...] + spread_cols(cols, num_ref.shape)
    attended = ((total[:, :width] + num_ref[...]) / den).astype(BF16)
    out_ref[...] = jnp.dot(attended, w_ref[...], preferred_element_type=F32).astype(BF16)


def final_kernel(tp_ref, *refs):
    *part_refs, rows_ref, rate_ref, short_ref, long_ref = refs
    n_short, width = short_ref.shape
    n_long = long_ref.shape[0]
    features = rows_ref.shape[1]
    proj = part_refs[0][...].astype(F32)
    for part in part_refs[1:]:
        proj = proj + part[...].astype(F32)
    proj = proj * lax.rsqrt(jnp.sum(proj * proj, -1, keepdims=True) / features + EPS)
    state = rows_ref[...].astype(F32)
    update = state + rate_ref[...] * (proj - state)
    square = jnp.sum(update * update, -1, keepdims=True)
    mine = update[:, :width]
    for t in range(1, features // width):
        mine = jnp.where(tp_ref[0] == t, update[:, t * width : (t + 1) * width], mine)
    result = (mine * lax.rsqrt(square / features + EPS)).astype(BF16)
    short_ref[...] = result[:n_short]
    long_ref[...] = result[n_short : n_short + n_long]


def sender(me, k, size):
    return me ^ k if size & (size - 1) == 0 else lax.rem(me - k + size, size)


def from_all(x, axis):
    size = lax.axis_size(axis)
    got = [x]
    for k in range(1, size):
        pairs = [(i, i ^ k if size & (size - 1) == 0 else (i + k) % size) for i in range(size)]
        got.append(lax.ppermute(x, axis, pairs))
    return got


VMEM = pl.BlockSpec(memory_space=pltpu.VMEM)
SMEM = pl.BlockSpec(memory_space=pltpu.SMEM)


def call(kernel, outs, ins, flops, moved, scratch=(), scalars=0, limit=16):
    return pl.pallas_call(
        kernel,
        out_shape=outs,
        in_specs=[SMEM] * scalars + [VMEM] * (len(ins) - scalars),
        out_specs=jax.tree.map(lambda _: VMEM, outs),
        scratch_shapes=scratch,
        compiler_params=pltpu.CompilerParams(vmem_limit_bytes=limit * 1024 * 1024),
        cost_estimate=pl.CostEstimate(flops=flops, bytes_accessed=moved, transcendentals=0),
    )(*ins)


def on_device(
    short_hidden,
    long_hidden,
    short_len,
    short_slot,
    w_query,
    w_key,
    w_value,
    w_out,
    qk_gain,
    step_rate,
    short_keys,
    short_values,
    long_keys,
    long_values,
):
    n_short, width = short_hidden.shape
    n_long = long_hidden.shape[0]
    groups = lax.axis_size("seq")
    features = w_query.shape[0]
    slots = short_keys.shape[0]
    total = short_len.shape[0]
    pad = -(n_short + n_long) % SUB
    count = n_short + n_long + pad
    sent_width = -(-(width + 2 * SUB) // 128) * 128
    out = jax.ShapeDtypeStruct

    w_query, w_key, w_value = w_query.T, w_key.T, w_value.T
    short_keys, short_values, long_keys, long_values = (
        jnp.swapaxes(a, 1, 2) for a in (short_keys, short_values, long_keys, long_values)
    )
    mine = jnp.concatenate([short_hidden, long_hidden, jnp.zeros((pad, width), BF16)], 0)
    pieces = from_all(mine, "tp")
    gain = qk_gain.reshape(1, width)
    position = short_slot - lax.axis_index("seq") * slots
    tp_index = lax.axis_index("tp").reshape(1)

    send, query, rows = call(
        query_kernel,
        (
            out((groups, n_short, width), BF16),
            out((count, width), BF16),
            out((count, features), BF16),
        ),
        (tp_index, *pieces, w_query, gain),
        2 * count * features * width,
        2 * features * width,
        scratch=[pltpu.VMEM((len(pieces), count, width), F32)],
        scalars=1,
    )
    queries = lax.all_to_all(send, "seq", split_axis=0, concat_axis=0, tiled=True)
    own_den, own_num, long_part = call(
        functools.partial(local_kernel, n_short),
        (out((count, width), F32), out((count, width), F32), out((count - n_short, sent_width), F32)),
        (rows, w_key, w_value, gain, query, long_keys, long_values),
        4 * count * features * width,
        4 * features * width + 4 * long_keys.size,
    )
    sent = call(
        short_kernel,
        out((groups, count, sent_width), BF16),
        (
            position.reshape(1, total),
            position.reshape(total, 1),
            short_len.reshape(1, total),
            queries,
            short_keys,
            short_values,
            long_part,
        ),
        4 * short_keys.size * SUB,
        4 * short_keys.size,
        scratch=[pltpu.VMEM((slots * SUB, sent_width), F32)],
    )
    back = lax.all_to_all(sent, "seq", split_axis=0, concat_axis=0, tiled=True)
    partial = call(
        combine_kernel,
        out((count, features), BF16),
        (back, own_den, own_num, w_out),
        2 * count * features * width,
        2 * features * width,
    )
    partials = from_all(partial, "tp")
    return call(
        final_kernel,
        (out((n_short, width), BF16), out((n_long, width), BF16)),
        (tp_index, *partials, rows, step_rate.reshape(1, features)),
        10 * count * features,
        10 * count * features,
        scalars=1,
    )


def solution(mesh):
    return jax.shard_map(
        on_device,
        mesh=mesh,
        in_specs=(
            P("seq", "tp"),
            P(None, "tp"),
            P(),
            P(),
            P(None, "tp"),
            P(None, "tp"),
            P(None, "tp"),
            P("tp", None),
            P("tp"),
            P(),
            P("seq", None, "tp"),
            P("seq", None, "tp"),
            P(None, "seq", "tp"),
            P(None, "seq", "tp"),
        ),
        out_specs=(P("seq", "tp"), P(None, "tp")),
        check_vma=False,
    )
```

```python
import functools
import math

import jax
import jax.numpy as jnp
from jax import lax
from jax.experimental import pallas as pl
from jax.experimental.pallas import tpu as pltpu
from jax.sharding import PartitionSpec as P

HEAD = 64
EPS = 1e-06
SUB = 8
BF16 = jnp.bfloat16
F32 = jnp.float32
NT = (((1,), (1,)), ((), ()))


def lanes(shape):
    return lax.broadcasted_iota(jnp.int32, shape, len(shape) - 1)


def rows_of(shape):
    return lax.broadcasted_iota(jnp.int32, shape, len(shape) - 2)


def head_cols(x):
    head = lanes(x.shape) // HEAD
    return [
        jnp.sum(jnp.where(head == h, x, 0.0), -1, keepdims=True)
        for h in range(x.shape[-1] // HEAD)
    ]


def spread_cols(cols, shape):
    head = lanes(shape) // HEAD
    out = jnp.broadcast_to(cols[0], shape)
    for h in range(1, len(cols)):
        out = jnp.where(head == h, cols[h], out)
    return out


def head_unit(x, gain):
    scale = spread_cols([lax.rsqrt(c + EPS) for c in head_cols(x * x)], x.shape)
    return x * scale * gain


def project(rows, w_ref):
    return lax.dot_general(rows, w_ref[...], NT, preferred_element_type=F32)


def prepare_kernel(base_ref, slot_ref, len_ref, hit_ref, spread_ref, live_ref):
    exp_rows, total = hit_ref.shape
    hit = slot_ref[...] - base_ref[0] == rows_of((exp_rows, total)) // SUB
    ones = jnp.where(hit, 1.0, 0.0)
    hit_ref[...] = ones.astype(BF16)
    spread_ref[...] = ones.T.astype(BF16)
    lengths = jnp.sum(jnp.where(hit, len_ref[...], 0), -1, keepdims=True)
    live_ref[...] = jnp.where(lanes(live_ref.shape) < lengths, 1.0, 0.0)


def sender(me, k, size):
    return me ^ k if size & (size - 1) == 0 else lax.rem(me - k + size, size)


def query_kernel(tp_ref, *refs):
    *piece_refs, w_ref, gain_ref, send_ref, query_ref, rows_ref, order_ref = refs
    for k, piece in enumerate(piece_refs):
        order_ref[sender(tp_ref[0], k, len(piece_refs))] = piece[...].astype(F32)
    rows = jnp.concatenate([order_ref[t] for t in range(len(piece_refs))], 1).astype(BF16)
    rows_ref[...] = rows
    query = head_unit(project(rows, w_ref), gain_ref[...]).astype(BF16)
    query_ref[...] = query
    groups, n_short, _ = send_ref.shape
    for g in range(groups):
        send_ref[g] = query[:n_short]


def den_tile(den, width):
    shape = (den.shape[0], width)
    high = den.astype(BF16).astype(F32)
    low = den - high
    lane, row = lanes(shape), rows_of(shape) % SUB
    return jnp.where(lane == row, high, jnp.where(lane == row + SUB, low, 0.0))


def local_kernel(n_short, rows_ref, wk_ref, wv_ref, gain_ref, q_ref, lk_ref, lv_ref, den_ref, num_ref, pay_ref):
    long_count, width, _ = lk_ref.shape
    heads = width // HEAD
    query = q_ref[...].astype(F32)
    rows = rows_ref[...]
    new_key = head_unit(project(rows, wk_ref), gain_ref[...]).astype(BF16).astype(F32)
    new_value = project(rows, wv_ref).astype(BF16).astype(F32)
    own = [jnp.exp(c * math.sqrt(HEAD)) for c in head_cols(query * new_key)]
    den_ref[...] = spread_cols(own, query.shape)
    num_ref[...] = (
        spread_cols([o.astype(BF16).astype(F32) for o in own], query.shape) * new_value
    )
    shape = (SUB, width)
    mask = (lanes(shape) // HEAD) == rows_of(shape)
    pay_ref[...] = jnp.zeros(pay_ref.shape, F32)
    tail = pay_ref.shape[1] - width
    for i in range(long_count):
        row = query[n_short + i : n_short + i + 1] * math.sqrt(HEAD)
        blocks = jnp.where(mask, jnp.broadcast_to(row, shape), 0.0).astype(BF16)
        weights = jnp.exp(jnp.dot(blocks, lk_ref[i], preferred_element_type=F32))
        den = jnp.sum(weights, -1, keepdims=True)
        num = lax.dot_general(weights.astype(BF16), lv_ref[i], NT, preferred_element_type=F32)
        pay_ref[i : i + 1, :width] = jnp.sum(jnp.where(mask, num, 0.0), 0, keepdims=True)
        pay_ref[i : i + 1, width:] = jnp.sum(
            jnp.where(rows_of((SUB, tail)) < heads, den_tile(den, tail), 0.0), 0, keepdims=True
        )


def short_kernel(hit_ref, spread_ref, live_ref, q_ref, k_ref, v_ref, long_ref, out_ref, score_ref, num_ref):
    slots, width, _ = k_ref.shape
    groups, n_short, _ = q_ref.shape
    total = groups * n_short
    heads = width // HEAD
    exp_rows = slots * SUB
    queries = q_ref[...].reshape(total, width)
    picked = jnp.dot(hit_ref[...], queries, preferred_element_type=F32)
    shape = (exp_rows, width)
    mask = (lanes(shape) // HEAD) == (rows_of(shape) % SUB)
    blocks = jnp.where(mask, picked * math.sqrt(HEAD), 0.0).astype(BF16)
    for s in range(slots):
        at = slice(s * SUB, (s + 1) * SUB)
        score_ref[at] = jnp.dot(blocks[at], k_ref[s], preferred_element_type=F32)
    weights = jnp.where(live_ref[...] > 0.0, jnp.exp(score_ref[...]), 0.0)
    den = jnp.sum(weights, -1, keepdims=True)
    rounded = weights.astype(BF16)
    for s in range(slots):
        at = slice(s * SUB, (s + 1) * SUB)
        num_ref[at] = lax.dot_general(rounded[at], v_ref[s], NT, preferred_element_type=F32)
    num = jnp.where(mask, num_ref[...], 0.0).astype(BF16)
    tail = out_ref.shape[-1] - width
    real = rows_of((exp_rows, tail)) % SUB < heads
    dens = jnp.where(real, den_tile(den, tail), 0.0).astype(BF16)
    spread = spread_ref[...]
    sent = jnp.dot(spread, num, preferred_element_type=F32).astype(BF16)
    out_ref[:, :n_short, :width] = sent.reshape(groups, n_short, width)
    sent = jnp.dot(spread, dens, preferred_element_type=F32).astype(BF16)
    out_ref[:, :n_short, width:] = sent.reshape(groups, n_short, tail)
    extra = long_ref[...].astype(BF16)
    for g in range(groups):
        out_ref[g, n_short:, :] = extra


def combine_kernel(back_ref, den_ref, num_ref, w_ref, out_ref):
    width = num_ref.shape[-1]
    heads = width // HEAD
    total = back_ref[0].astype(F32)
    for g in range(1, back_ref.shape[0]):
        total = total + back_ref[g].astype(F32)
    dens = total[:, width:]
    cols = [dens[:, h : h + 1] + dens[:, SUB + h : SUB + h + 1] for h in range(heads)]
    den = den_ref[...] + spread_cols(cols, num_ref.shape)
    attended = ((total[:, :width] + num_ref[...]) / den).astype(BF16)
    out_ref[...] = jnp.dot(attended, w_ref[...], preferred_element_type=F32).astype(BF16)


def final_kernel(tp_ref, *refs):
    *part_refs, rows_ref, rate_ref, short_ref, long_ref = refs
    n_short, width = short_ref.shape
    n_long = long_ref.shape[0]
    features = rows_ref.shape[1]
    proj = part_refs[0][...].astype(F32)
    for part in part_refs[1:]:
        proj = proj + part[...].astype(F32)
    proj = proj * lax.rsqrt(jnp.sum(proj * proj, -1, keepdims=True) / features + EPS)
    state = rows_ref[...].astype(F32)
    update = state + rate_ref[...] * (proj - state)
    square = jnp.sum(update * update, -1, keepdims=True)
    mine = update[:, :width]
    for t in range(1, features // width):
        mine = jnp.where(tp_ref[0] == t, update[:, t * width : (t + 1) * width], mine)
    result = (mine * lax.rsqrt(square / features + EPS)).astype(BF16)
    short_ref[...] = result[:n_short]
    long_ref[...] = result[n_short : n_short + n_long]


def size_of(axis):
    return lax.axis_size(axis)


def from_all(x, axis):
    size = size_of(axis)
    got = [x]
    for k in range(1, size):
        pairs = [(i, i ^ k if size & (size - 1) == 0 else (i + k) % size) for i in range(size)]
        got.append(lax.ppermute(x, axis, pairs))
    return got


def exchange(x, axis):
    return lax.all_to_all(x, axis, split_axis=0, concat_axis=0, tiled=True)


VMEM = pl.BlockSpec(memory_space=pltpu.VMEM)
SMEM = pl.BlockSpec(memory_space=pltpu.SMEM)


def call(kernel, outs, ins, flops, moved, scratch=(), scalars=0, limit=16):
    return pl.pallas_call(
        kernel,
        out_shape=outs,
        in_specs=[SMEM] * scalars + [VMEM] * (len(ins) - scalars),
        out_specs=jax.tree.map(lambda _: VMEM, outs),
        scratch_shapes=scratch,
        compiler_params=pltpu.CompilerParams(vmem_limit_bytes=limit * 1024 * 1024),
        cost_estimate=pl.CostEstimate(flops=flops, bytes_accessed=moved, transcendentals=0),
    )(*ins)


def on_device(
    short_hidden,
    long_hidden,
    short_len,
    short_slot,
    w_query,
    w_key,
    w_value,
    w_out,
    qk_gain,
    step_rate,
    short_keys,
    short_values,
    long_keys,
    long_values,
):
    n_short, width = short_hidden.shape
    n_long = long_hidden.shape[0]
    groups = size_of("seq")
    features = w_query.shape[0]
    slots, capacity, _ = short_keys.shape
    total = short_len.shape[0]
    pad = -(n_short + n_long) % SUB
    count = n_short + n_long + pad
    sent_width = -(-(width + 2 * SUB) // 128) * 128
    out = jax.ShapeDtypeStruct
    tp_index = lax.axis_index("tp").reshape(1)
    base = (lax.axis_index("seq") * slots).reshape(1)

    mine = jnp.concatenate([short_hidden, long_hidden, jnp.zeros((pad, width), BF16)], 0)
    pieces = from_all(mine, "tp")
    gain = qk_gain.reshape(1, width)
    w_query, w_key, w_value = w_query.T, w_key.T, w_value.T
    short_keys, short_values, long_keys, long_values = (
        jnp.swapaxes(a, 1, 2) for a in (short_keys, short_values, long_keys, long_values)
    )
    hit, spread, live = call(
        prepare_kernel,
        (
            out((slots * SUB, total), BF16),
            out((total, slots * SUB), BF16),
            out((slots * SUB, capacity), F32),
        ),
        (base, short_slot.reshape(1, total), short_len.reshape(1, total)),
        10**11,
        slots * SUB * total,
        scalars=1,
    )
    send, query, rows = call(
        query_kernel,
        (
            out((groups, n_short, width), BF16),
            out((count, width), BF16),
            out((count, features), BF16),
        ),
        (tp_index, *pieces, w_query, gain),
        10**11,
        2 * features * width,
        scratch=[pltpu.VMEM((len(pieces), count, width), F32)],
        scalars=1,
    )
    queries = exchange(send, "seq")
    own_den, own_num, long_part = call(
        functools.partial(local_kernel, n_short),
        (out((count, width), F32), out((count, width), F32), out((count - n_short, sent_width), F32)),
        (rows, w_key, w_value, gain, query, long_keys, long_values),
        10**8,
        4 * features * width + 4 * long_keys.size,
    )
    sent = call(
        short_kernel,
        out((groups, count, sent_width), BF16),
        (hit, spread, live, queries, short_keys, short_values, long_part),
        4 * short_keys.size * SUB,
        4 * short_keys.size,
        scratch=[pltpu.VMEM((slots * SUB, capacity), F32), pltpu.VMEM((slots * SUB, width), F32)],
    )
    back = exchange(sent, "seq")
    partial = call(
        combine_kernel,
        out((count, features), BF16),
        (back, own_den, own_num, w_out),
        2 * count * features * width,
        2 * features * width,
    )
    partials = from_all(partial, "tp")
    return call(
        final_kernel,
        (out((n_short, width), BF16), out((n_long, width), BF16)),
        (tp_index, *partials, rows, step_rate.reshape(1, features)),
        10 * count * features,
        10 * count * features,
        scalars=1,
    )


def solution(mesh):
    return jax.shard_map(
        on_device,
        mesh=mesh,
        in_specs=(
            P("seq", "tp"),
            P(None, "tp"),
            P(),
            P(),
            P(None, "tp"),
            P(None, "tp"),
            P(None, "tp"),
            P("tp", None),
            P("tp"),
            P(),
            P("seq", None, "tp"),
            P("seq", None, "tp"),
            P(None, "seq", "tp"),
            P(None, "seq", "tp"),
        ),
        out_specs=(P("seq", "tp"), P(None, "tp")),
        check_vma=False,
    )
```

```python
import functools
import math

import jax
import jax.numpy as jnp
from jax import lax
from jax.experimental import pallas as pl
from jax.experimental.pallas import tpu as pltpu
from jax.sharding import PartitionSpec as P

HEAD = 64
EPS = 1e-06
SUB = 8
BF16 = jnp.bfloat16
F32 = jnp.float32
NT = (((1,), (1,)), ((), ()))


def lanes(shape):
    return lax.broadcasted_iota(jnp.int32, shape, len(shape) - 1)


def rows_of(shape):
    return lax.broadcasted_iota(jnp.int32, shape, len(shape) - 2)


def head_cols(x):
    head = lanes(x.shape) // HEAD
    return [
        jnp.sum(jnp.where(head == h, x, 0.0), -1, keepdims=True)
        for h in range(x.shape[-1] // HEAD)
    ]


def spread_cols(cols, shape):
    head = lanes(shape) // HEAD
    out = jnp.broadcast_to(cols[0], shape)
    for h in range(1, len(cols)):
        out = jnp.where(head == h, cols[h], out)
    return out


def head_unit(x, gain):
    scale = spread_cols([lax.rsqrt(c + EPS) for c in head_cols(x * x)], x.shape)
    return x * scale * gain


def project(rows, w_ref):
    return lax.dot_general(rows, w_ref[...], NT, preferred_element_type=F32)


def prepare_kernel(base_ref, slot_ref, len_ref, gain_ref, hit_ref, spread_ref, live_ref, row_ref):
    row_ref[...] = gain_ref[...]
    exp_rows, total = hit_ref.shape
    hit = slot_ref[...] - base_ref[0] == rows_of((exp_rows, total)) // SUB
    ones = jnp.where(hit, 1.0, 0.0)
    hit_ref[...] = ones.astype(BF16)
    spread_ref[...] = ones.T.astype(BF16)
    lengths = jnp.sum(jnp.where(hit, len_ref[...], 0), -1, keepdims=True)
    live_ref[...] = jnp.where(lanes(live_ref.shape) < lengths, 1.0, 0.0)


def sender(me, k, size):
    return me ^ k if size & (size - 1) == 0 else lax.rem(me - k + size, size)


def query_kernel(tp_ref, *refs):
    *piece_refs, w_ref, gain_ref, send_ref, query_ref, rows_ref, order_ref = refs
    for k, piece in enumerate(piece_refs):
        order_ref[sender(tp_ref[0], k, len(piece_refs))] = piece[...].astype(F32)
    rows = jnp.concatenate([order_ref[t] for t in range(len(piece_refs))], 1).astype(BF16)
    rows_ref[...] = rows
    query = head_unit(project(rows, w_ref), gain_ref[...]).astype(BF16)
    query_ref[...] = query
    groups, n_short, _ = send_ref.shape
    for g in range(groups):
        send_ref[g] = query[:n_short]


def den_tile(den, width):
    shape = (den.shape[0], width)
    high = den.astype(BF16).astype(F32)
    low = den - high
    lane, row = lanes(shape), rows_of(shape) % SUB
    return jnp.where(lane == row, high, jnp.where(lane == row + SUB, low, 0.0))


def local_kernel(n_short, rows_ref, wk_ref, wv_ref, gain_ref, q_ref, lk_ref, lv_ref, den_ref, num_ref, pay_ref):
    long_count, width, _ = lk_ref.shape
    heads = width // HEAD
    query = q_ref[...].astype(F32)
    rows = rows_ref[...]
    new_key = head_unit(project(rows, wk_ref), gain_ref[...]).astype(BF16).astype(F32)
    new_value = project(rows, wv_ref).astype(BF16).astype(F32)
    own = [jnp.exp(c * math.sqrt(HEAD)) for c in head_cols(query * new_key)]
    den_ref[...] = spread_cols(own, query.shape)
    num_ref[...] = (
        spread_cols([o.astype(BF16).astype(F32) for o in own], query.shape) * new_value
    )
    shape = (SUB, width)
    mask = (lanes(shape) // HEAD) == rows_of(shape)
    pay_ref[...] = jnp.zeros(pay_ref.shape, F32)
    tail = pay_ref.shape[1] - width
    for i in range(long_count):
        row = query[n_short + i : n_short + i + 1] * math.sqrt(HEAD)
        blocks = jnp.where(mask, jnp.broadcast_to(row, shape), 0.0).astype(BF16)
        weights = jnp.exp(jnp.dot(blocks, lk_ref[i], preferred_element_type=F32))
        den = jnp.sum(weights, -1, keepdims=True)
        num = lax.dot_general(weights.astype(BF16), lv_ref[i], NT, preferred_element_type=F32)
        pay_ref[i : i + 1, :width] = jnp.sum(jnp.where(mask, num, 0.0), 0, keepdims=True)
        pay_ref[i : i + 1, width:] = jnp.sum(
            jnp.where(rows_of((SUB, tail)) < heads, den_tile(den, tail), 0.0), 0, keepdims=True
        )


def short_kernel(hit_ref, spread_ref, live_ref, q_ref, k_ref, v_ref, long_ref, out_ref, score_ref, num_ref):
    slots, width, _ = k_ref.shape
    groups, n_short, _ = q_ref.shape
    total = groups * n_short
    heads = width // HEAD
    exp_rows = slots * SUB
    queries = q_ref[...].reshape(total, width)
    picked = jnp.dot(hit_ref[...], queries, preferred_element_type=F32)
    shape = (exp_rows, width)
    mask = (lanes(shape) // HEAD) == (rows_of(shape) % SUB)
    blocks = jnp.where(mask, picked * math.sqrt(HEAD), 0.0).astype(BF16)
    for s in range(slots):
        at = slice(s * SUB, (s + 1) * SUB)
        score_ref[at] = jnp.dot(blocks[at], k_ref[s], preferred_element_type=F32)
    weights = jnp.where(live_ref[...] > 0.0, jnp.exp(score_ref[...]), 0.0)
    den = jnp.sum(weights, -1, keepdims=True)
    rounded = weights.astype(BF16)
    for s in range(slots):
        at = slice(s * SUB, (s + 1) * SUB)
        num_ref[at] = lax.dot_general(rounded[at], v_ref[s], NT, preferred_element_type=F32)
    num = jnp.where(mask, num_ref[...], 0.0).astype(BF16)
    tail = out_ref.shape[-1] - width
    real = rows_of((exp_rows, tail)) % SUB < heads
    dens = jnp.where(real, den_tile(den, tail), 0.0).astype(BF16)
    spread = spread_ref[...]
    sent = jnp.dot(spread, num, preferred_element_type=F32).astype(BF16)
    out_ref[:, :n_short, :width] = sent.reshape(groups, n_short, width)
    sent = jnp.dot(spread, dens, preferred_element_type=F32).astype(BF16)
    out_ref[:, :n_short, width:] = sent.reshape(groups, n_short, tail)
    extra = long_ref[...].astype(BF16)
    for g in range(groups):
        out_ref[g, n_short:, :] = extra


def combine_kernel(back_ref, den_ref, num_ref, w_ref, out_ref):
    width = num_ref.shape[-1]
    heads = width // HEAD
    total = back_ref[0].astype(F32)
    for g in range(1, back_ref.shape[0]):
        total = total + back_ref[g].astype(F32)
    dens = total[:, width:]
    cols = [dens[:, h : h + 1] + dens[:, SUB + h : SUB + h + 1] for h in range(heads)]
    den = den_ref[...] + spread_cols(cols, num_ref.shape)
    attended = ((total[:, :width] + num_ref[...]) / den).astype(BF16)
    out_ref[...] = jnp.dot(attended, w_ref[...], preferred_element_type=F32).astype(BF16)


def final_kernel(tp_ref, *refs):
    *part_refs, rows_ref, rate_ref, short_ref, long_ref = refs
    n_short, width = short_ref.shape
    n_long = long_ref.shape[0]
    features = rows_ref.shape[1]
    proj = part_refs[0][...].astype(F32)
    for part in part_refs[1:]:
        proj = proj + part[...].astype(F32)
    proj = proj * lax.rsqrt(jnp.sum(proj * proj, -1, keepdims=True) / features + EPS)
    state = rows_ref[...].astype(F32)
    update = state + rate_ref[...] * (proj - state)
    square = jnp.sum(update * update, -1, keepdims=True)
    mine = update[:, :width]
    for t in range(1, features // width):
        mine = jnp.where(tp_ref[0] == t, update[:, t * width : (t + 1) * width], mine)
    result = (mine * lax.rsqrt(square / features + EPS)).astype(BF16)
    short_ref[...] = result[:n_short]
    long_ref[...] = result[n_short : n_short + n_long]


def size_of(axis):
    return lax.axis_size(axis)


def from_all(x, axis):
    size = size_of(axis)
    got = [x]
    for k in range(1, size):
        pairs = [(i, i ^ k if size & (size - 1) == 0 else (i + k) % size) for i in range(size)]
        got.append(lax.ppermute(x, axis, pairs))
    return got


def exchange(x, axis):
    return lax.all_to_all(x, axis, split_axis=0, concat_axis=0, tiled=True)


VMEM = pl.BlockSpec(memory_space=pltpu.VMEM)
SMEM = pl.BlockSpec(memory_space=pltpu.SMEM)


def call(kernel, outs, ins, flops, moved, scratch=(), scalars=0, limit=16):
    return pl.pallas_call(
        kernel,
        out_shape=outs,
        in_specs=[SMEM] * scalars + [VMEM] * (len(ins) - scalars),
        out_specs=jax.tree.map(lambda _: VMEM, outs),
        scratch_shapes=scratch,
        compiler_params=pltpu.CompilerParams(vmem_limit_bytes=limit * 1024 * 1024),
        cost_estimate=pl.CostEstimate(flops=flops, bytes_accessed=moved, transcendentals=0),
    )(*ins)


def on_device(
    short_hidden,
    long_hidden,
    short_len,
    short_slot,
    w_query,
    w_key,
    w_value,
    w_out,
    qk_gain,
    step_rate,
    short_keys,
    short_values,
    long_keys,
    long_values,
):
    n_short, width = short_hidden.shape
    n_long = long_hidden.shape[0]
    groups = size_of("seq")
    features = w_query.shape[0]
    slots, capacity, _ = short_keys.shape
    total = short_len.shape[0]
    pad = -(n_short + n_long) % SUB
    count = n_short + n_long + pad
    sent_width = -(-(width + 2 * SUB) // 128) * 128
    out = jax.ShapeDtypeStruct
    tp_index = lax.axis_index("tp").reshape(1)
    base = (lax.axis_index("seq") * slots).reshape(1)

    mine = jnp.concatenate([short_hidden, long_hidden, jnp.zeros((pad, width), BF16)], 0)
    pieces = from_all(mine, "tp")
    w_query, w_key, w_value = w_query.T, w_key.T, w_value.T
    short_keys, short_values, long_keys, long_values = (
        jnp.swapaxes(a, 1, 2) for a in (short_keys, short_values, long_keys, long_values)
    )
    hit, spread, live, gain = call(
        prepare_kernel,
        (
            out((slots * SUB, total), BF16),
            out((total, slots * SUB), BF16),
            out((slots * SUB, capacity), F32),
            out((1, width), F32),
        ),
        (base, short_slot.reshape(1, total), short_len.reshape(1, total), qk_gain.reshape(1, width)),
        10**11,
        slots * SUB * total,
        scalars=1,
    )
    send, query, rows = call(
        query_kernel,
        (
            out((groups, n_short, width), BF16),
            out((count, width), BF16),
            out((count, features), BF16),
        ),
        (tp_index, *pieces, w_query, gain),
        10**11,
        2 * features * width,
        scratch=[pltpu.VMEM((len(pieces), count, width), F32)],
        scalars=1,
    )
    queries = exchange(send, "seq")
    own_den, own_num, long_part = call(
        functools.partial(local_kernel, n_short),
        (out((count, width), F32), out((count, width), F32), out((count - n_short, sent_width), F32)),
        (rows, w_key, w_value, gain, query, long_keys, long_values),
        10**8,
        4 * features * width + 4 * long_keys.size,
    )
    sent = call(
        short_kernel,
        out((groups, count, sent_width), BF16),
        (hit, spread, live, queries, short_keys, short_values, long_part),
        4 * short_keys.size * SUB,
        4 * short_keys.size,
        scratch=[pltpu.VMEM((slots * SUB, capacity), F32), pltpu.VMEM((slots * SUB, width), F32)],
    )
    back = exchange(sent, "seq")
    partial = call(
        combine_kernel,
        out((count, features), BF16),
        (back, own_den, own_num, w_out),
        2 * count * features * width,
        2 * features * width,
    )
    partials = from_all(partial, "tp")
    return call(
        final_kernel,
        (out((n_short, width), BF16), out((n_long, width), BF16)),
        (tp_index, *partials, rows, step_rate.reshape(1, features)),
        10 * count * features,
        10 * count * features,
        scalars=1,
    )


def solution(mesh):
    return jax.shard_map(
        on_device,
        mesh=mesh,
        in_specs=(
            P("seq", "tp"),
            P(None, "tp"),
            P(),
            P(),
            P(None, "tp"),
            P(None, "tp"),
            P(None, "tp"),
            P("tp", None),
            P("tp"),
            P(),
            P("seq", None, "tp"),
            P("seq", None, "tp"),
            P(None, "seq", "tp"),
            P(None, "seq", "tp"),
        ),
        out_specs=(P("seq", "tp"), P(None, "tp")),
        check_vma=False,
    )
```

```python
import functools
import math

import jax
import jax.numpy as jnp
from jax import lax
from jax.experimental import pallas as pl
from jax.experimental.pallas import tpu as pltpu
from jax.sharding import PartitionSpec as P

HEAD = 64
EPS = 1e-06
SUB = 8
BF16 = jnp.bfloat16
F32 = jnp.float32
NT = (((1,), (1,)), ((), ()))


def lanes(shape):
    return lax.broadcasted_iota(jnp.int32, shape, len(shape) - 1)


def rows_of(shape):
    return lax.broadcasted_iota(jnp.int32, shape, len(shape) - 2)


def head_cols(x):
    head = lanes(x.shape) // HEAD
    return [
        jnp.sum(jnp.where(head == h, x, 0.0), -1, keepdims=True)
        for h in range(x.shape[-1] // HEAD)
    ]


def spread_cols(cols, shape):
    head = lanes(shape) // HEAD
    out = jnp.broadcast_to(cols[0], shape)
    for h in range(1, len(cols)):
        out = jnp.where(head == h, cols[h], out)
    return out


def head_unit(x, gain):
    scale = spread_cols([lax.rsqrt(c + EPS) for c in head_cols(x * x)], x.shape)
    return x * scale * gain


def project(rows, w_ref):
    return lax.dot_general(rows, w_ref[...], NT, preferred_element_type=F32)


def prepare_kernel(base_ref, slot_ref, len_ref, hit_ref, spread_ref, live_ref):
    exp_rows, total = hit_ref.shape
    hit = slot_ref[...] - base_ref[0] == rows_of((exp_rows, total)) // SUB
    ones = jnp.where(hit, 1.0, 0.0)
    hit_ref[...] = ones.astype(BF16)
    spread_ref[...] = ones.T.astype(BF16)
    lengths = jnp.sum(jnp.where(hit, len_ref[...], 0), -1, keepdims=True)
    live_ref[...] = jnp.where(lanes(live_ref.shape) < lengths, 1.0, 0.0)


def gain_kernel(gain_ref, row_ref):
    row_ref[...] = gain_ref[...]


def sender(me, place, size):
    k = (size - place) % size
    return me ^ k if size & (size - 1) == 0 else lax.rem(me - k + size, size)


def query_kernel(tp_ref, *refs):
    *piece_refs, w_ref, gain_ref, send_ref, query_ref, rows_ref, order_ref = refs
    for k, piece in enumerate(piece_refs):
        order_ref[sender(tp_ref[0], k, len(piece_refs))] = piece[...].astype(F32)
    rows = jnp.concatenate([order_ref[t] for t in range(len(piece_refs))], 1).astype(BF16)
    rows_ref[...] = rows
    query = head_unit(project(rows, w_ref), gain_ref[...]).astype(BF16)
    query_ref[...] = query
    groups, n_short, _ = send_ref.shape
    for g in range(groups):
        send_ref[g] = query[:n_short]


def den_tile(den, width):
    shape = (den.shape[0], width)
    high = den.astype(BF16).astype(F32)
    low = den - high
    lane, row = lanes(shape), rows_of(shape) % SUB
    return jnp.where(lane == row, high, jnp.where(lane == row + SUB, low, 0.0))


def long_kernel(n_short, q_ref, k_ref, v_ref, pay_ref):
    long_count, width, _ = k_ref.shape
    heads = width // HEAD
    query = q_ref[...].astype(F32)
    shape = (SUB, width)
    mask = (lanes(shape) // HEAD) == rows_of(shape)
    weights = []
    for i in range(long_count):
        row = query[n_short + i : n_short + i + 1] * math.sqrt(HEAD)
        blocks = jnp.where(mask, jnp.broadcast_to(row, shape), 0.0).astype(BF16)
        weights.append(jnp.exp(jnp.dot(blocks, k_ref[i], preferred_element_type=F32)))
    pay_ref[...] = jnp.zeros(pay_ref.shape, F32)
    tail = pay_ref.shape[1] - width
    real = rows_of((SUB, tail)) < heads
    for i in range(long_count):
        den = jnp.sum(weights[i], -1, keepdims=True)
        num = lax.dot_general(weights[i].astype(BF16), v_ref[i], NT, preferred_element_type=F32)
        pay_ref[i : i + 1, :width] = jnp.sum(jnp.where(mask, num, 0.0), 0, keepdims=True)
        pay_ref[i : i + 1, width:] = jnp.sum(
            jnp.where(real, den_tile(den, tail), 0.0), 0, keepdims=True
        )


def own_kernel(rows_ref, wk_ref, wv_ref, gain_ref, q_ref, pay_ref, den_ref, num_ref, out_ref):
    out_ref[...] = pay_ref[...].astype(BF16)
    query = q_ref[...].astype(F32)
    rows = rows_ref[...]
    new_key = head_unit(project(rows, wk_ref), gain_ref[...]).astype(BF16).astype(F32)
    new_value = project(rows, wv_ref).astype(BF16).astype(F32)
    own = [jnp.exp(c * math.sqrt(HEAD)) for c in head_cols(query * new_key)]
    den_ref[...] = spread_cols(own, query.shape)
    num_ref[...] = (
        spread_cols([o.astype(BF16).astype(F32) for o in own], query.shape) * new_value
    )


def score_kernel(hit_ref, live_ref, q_ref, k_ref, weight_ref, den_ref, score_ref):
    slots, width, _ = k_ref.shape
    groups, n_short, _ = q_ref.shape
    exp_rows = slots * SUB
    queries = q_ref[...].reshape(groups * n_short, width)
    picked = jnp.dot(hit_ref[...], queries, preferred_element_type=F32)
    shape = (exp_rows, width)
    mask = (lanes(shape) // HEAD) == (rows_of(shape) % SUB)
    blocks = jnp.where(mask, picked * math.sqrt(HEAD), 0.0).astype(BF16)
    for s in range(slots):
        at = slice(s * SUB, (s + 1) * SUB)
        score_ref[at] = jnp.dot(blocks[at], k_ref[s], preferred_element_type=F32)
    weights = jnp.where(live_ref[...] > 0.0, jnp.exp(score_ref[...]), 0.0)
    weight_ref[...] = weights.astype(BF16)
    real = rows_of(den_ref.shape) % SUB < width // HEAD
    dens = den_tile(jnp.sum(weights, -1, keepdims=True), den_ref.shape[1])
    den_ref[...] = jnp.where(real, dens, 0.0).astype(BF16)


def value_kernel(spread_ref, weight_ref, den_ref, v_ref, long_ref, out_ref, num_ref):
    slots, width, _ = v_ref.shape
    groups, count, _ = out_ref.shape
    n_short = spread_ref.shape[0] // groups
    for s in range(slots):
        at = slice(s * SUB, (s + 1) * SUB)
        num_ref[at] = lax.dot_general(weight_ref[at], v_ref[s], NT, preferred_element_type=F32)
    shape = (slots * SUB, width)
    mask = (lanes(shape) // HEAD) == (rows_of(shape) % SUB)
    num = jnp.where(mask, num_ref[...], 0.0).astype(BF16)
    spread = spread_ref[...]
    sent = jnp.dot(spread, num, preferred_element_type=F32).astype(BF16)
    out_ref[:, :n_short, :width] = sent.reshape(groups, n_short, width)
    sent = jnp.dot(spread, den_ref[...], preferred_element_type=F32).astype(BF16)
    out_ref[:, :n_short, width:] = sent.reshape(groups, n_short, den_ref.shape[1])
    extra = long_ref[...]
    for g in range(groups):
        out_ref[g, n_short:, :] = extra


def combine_kernel(back_ref, den_ref, num_ref, w_ref, out_ref):
    width = num_ref.shape[-1]
    heads = width // HEAD
    total = back_ref[0].astype(F32)
    for g in range(1, back_ref.shape[0]):
        total = total + back_ref[g].astype(F32)
    dens = total[:, width:]
    cols = [dens[:, h : h + 1] + dens[:, SUB + h : SUB + h + 1] for h in range(heads)]
    den = den_ref[...] + spread_cols(cols, num_ref.shape)
    attended = ((total[:, :width] + num_ref[...]) / den).astype(BF16)
    out_ref[...] = jnp.dot(attended, w_ref[...], preferred_element_type=F32).astype(BF16)


def final_kernel(tp_ref, *refs):
    *part_refs, rows_ref, rate_ref, short_ref, long_ref = refs
    n_short, width = short_ref.shape
    n_long = long_ref.shape[0]
    features = rows_ref.shape[1]
    proj = part_refs[0][...].astype(F32)
    for part in part_refs[1:]:
        proj = proj + part[...].astype(F32)
    proj = proj * lax.rsqrt(jnp.sum(proj * proj, -1, keepdims=True) / features + EPS)
    state = rows_ref[...].astype(F32)
    update = state + rate_ref[...] * (proj - state)
    square = jnp.sum(update * update, -1, keepdims=True)
    mine = update[:, :width]
    for t in range(1, features // width):
        mine = jnp.where(tp_ref[0] == t, update[:, t * width : (t + 1) * width], mine)
    result = (mine * lax.rsqrt(square / features + EPS)).astype(BF16)
    short_ref[...] = result[:n_short]
    long_ref[...] = result[n_short : n_short + n_long]


def size_of(axis):
    return lax.axis_size(axis)


def from_all(x, axis):
    size = size_of(axis)
    got = []
    for k in range(size - 1, 0, -1):
        pairs = [(i, i ^ k if size & (size - 1) == 0 else (i + k) % size) for i in range(size)]
        got.append(lax.ppermute(x, axis, pairs))
    return [x, *got]


def exchange(x, axis):
    return lax.all_to_all(x, axis, split_axis=0, concat_axis=0, tiled=True)


VMEM = pl.BlockSpec(memory_space=pltpu.VMEM)
SMEM = pl.BlockSpec(memory_space=pltpu.SMEM)


def call(kernel, outs, ins, flops, moved, scratch=(), scalars=0, limit=16):
    return pl.pallas_call(
        kernel,
        out_shape=outs,
        in_specs=[SMEM] * scalars + [VMEM] * (len(ins) - scalars),
        out_specs=jax.tree.map(lambda _: VMEM, outs),
        scratch_shapes=scratch,
        compiler_params=pltpu.CompilerParams(vmem_limit_bytes=limit * 1024 * 1024),
        cost_estimate=pl.CostEstimate(flops=flops, bytes_accessed=moved, transcendentals=0),
    )(*ins)


def on_device(
    short_hidden,
    long_hidden,
    short_len,
    short_slot,
    w_query,
    w_key,
    w_value,
    w_out,
    qk_gain,
    step_rate,
    short_keys,
    short_values,
    long_keys,
    long_values,
):
    n_short, width = short_hidden.shape
    n_long = long_hidden.shape[0]
    groups = size_of("seq")
    features = w_query.shape[0]
    slots, capacity, _ = short_keys.shape
    total = short_len.shape[0]
    pad = -(n_short + n_long) % SUB
    count = n_short + n_long + pad
    sent_width = -(-(width + 2 * SUB) // 128) * 128
    out = jax.ShapeDtypeStruct
    tp_index = lax.axis_index("tp").reshape(1)
    base = (lax.axis_index("seq") * slots).reshape(1)

    mine = jnp.concatenate([short_hidden, long_hidden, jnp.zeros((pad, width), BF16)], 0)
    pieces = from_all(mine, "tp")
    gain = call(
        gain_kernel,
        out((1, width), F32),
        (qk_gain.reshape(1, width),),
        10**10,
        width,
    )
    w_query, w_key, w_value = w_query.T, w_key.T, w_value.T
    short_keys, short_values, long_keys, long_values = (
        jnp.swapaxes(a, 1, 2) for a in (short_keys, short_values, long_keys, long_values)
    )
    hit, spread, live = call(
        prepare_kernel,
        (
            out((slots * SUB, total), BF16),
            out((total, slots * SUB), BF16),
            out((slots * SUB, capacity), F32),
        ),
        (base, short_slot.reshape(1, total), short_len.reshape(1, total)),
        10**11,
        slots * SUB * total,
        scalars=1,
    )
    send, query, rows = call(
        query_kernel,
        (
            out((groups, n_short, width), BF16),
            out((count, width), BF16),
            out((count, features), BF16),
        ),
        (tp_index, *pieces, w_query, gain),
        10**11,
        2 * features * width,
        scratch=[pltpu.VMEM((len(pieces), count, width), F32)],
        scalars=1,
    )
    queries = exchange(send, "seq")
    long_part = call(
        functools.partial(long_kernel, n_short),
        out((count - n_short, sent_width), F32),
        (query, long_keys, long_values),
        10**8,
        4 * long_keys.size,
    )
    own_den, own_num, long_part = call(
        own_kernel,
        (
            out((count, width), F32),
            out((count, width), F32),
            out((count - n_short, sent_width), BF16),
        ),
        (rows, w_key, w_value, gain, query, long_part),
        10**9,
        4 * features * width,
    )
    weights, dens = call(
        score_kernel,
        (out((slots * SUB, capacity), BF16), out((slots * SUB, sent_width - width), BF16)),
        (hit, live, queries, short_keys),
        10**8,
        2 * short_keys.size,
        scratch=[pltpu.VMEM((slots * SUB, capacity), F32)],
    )
    sent = call(
        value_kernel,
        out((groups, count, sent_width), BF16),
        (spread, weights, dens, short_values, long_part),
        10**8,
        2 * short_values.size,
        scratch=[pltpu.VMEM((slots * SUB, width), F32)],
    )
    back = exchange(sent, "seq")
    partial = call(
        combine_kernel,
        out((count, features), BF16),
        (back, own_den, own_num, w_out),
        2 * count * features * width,
        2 * features * width,
    )
    partials = from_all(partial, "tp")
    return call(
        final_kernel,
        (out((n_short, width), BF16), out((n_long, width), BF16)),
        (tp_index, *partials, rows, step_rate.reshape(1, features)),
        10 * count * features,
        10 * count * features,
        scalars=1,
    )


def solution(mesh):
    return jax.shard_map(
        on_device,
        mesh=mesh,
        in_specs=(
            P("seq", "tp"),
            P(None, "tp"),
            P(),
            P(),
            P(None, "tp"),
            P(None, "tp"),
            P(None, "tp"),
            P("tp", None),
            P("tp"),
            P(),
            P("seq", None, "tp"),
            P("seq", None, "tp"),
            P(None, "seq", "tp"),
            P(None, "seq", "tp"),
        ),
        out_specs=(P("seq", "tp"), P(None, "tp")),
        check_vma=False,
    )
```

```python
import functools
import math

import jax
import jax.numpy as jnp
from jax import lax
from jax.experimental import pallas as pl
from jax.experimental.pallas import tpu as pltpu
from jax.sharding import PartitionSpec as P

HEAD = 64
EPS = 1e-06
SUB = 8
BF16 = jnp.bfloat16
F32 = jnp.float32
NT = (((1,), (1,)), ((), ()))


def lanes(shape):
    return lax.broadcasted_iota(jnp.int32, shape, len(shape) - 1)


def rows_of(shape):
    return lax.broadcasted_iota(jnp.int32, shape, len(shape) - 2)


def head_cols(x):
    head = lanes(x.shape) // HEAD
    return [
        jnp.sum(jnp.where(head == h, x, 0.0), -1, keepdims=True)
        for h in range(x.shape[-1] // HEAD)
    ]


def spread_cols(cols, shape):
    head = lanes(shape) // HEAD
    out = jnp.broadcast_to(cols[0], shape)
    for h in range(1, len(cols)):
        out = jnp.where(head == h, cols[h], out)
    return out


def head_unit(x, gain):
    scale = spread_cols([lax.rsqrt(c + EPS) for c in head_cols(x * x)], x.shape)
    return x * scale * gain


def project(rows, w_ref):
    return lax.dot_general(rows, w_ref[...], NT, preferred_element_type=F32)


def gain_kernel(gain_ref, row_ref):
    row_ref[...] = gain_ref[...]


def prepare_kernel(base_ref, slot_ref, len_ref, gain_ref, hit_ref, spread_ref, live_ref, row_ref):
    row_ref[...] = gain_ref[...]
    exp_rows, total = hit_ref.shape
    hit = slot_ref[...] - base_ref[0] == rows_of((exp_rows, total)) // SUB
    ones = jnp.where(hit, 1.0, 0.0)
    hit_ref[...] = ones.astype(BF16)
    spread_ref[...] = ones.T.astype(BF16)
    lengths = jnp.sum(jnp.where(hit, len_ref[...], 0), -1, keepdims=True)
    live_ref[...] = jnp.where(lanes(live_ref.shape) < lengths, 1.0, 0.0)


def sender(me, place, size):
    k = (size - place) % size
    return me ^ k if size & (size - 1) == 0 else lax.rem(me - k + size, size)


def query_kernel(tp_ref, *refs):
    *piece_refs, wq_ref, wk_ref, wv_ref, gain_ref, send_ref, query_ref, rows_ref, den_ref, num_ref, order_ref = refs
    for k, piece in enumerate(piece_refs):
        order_ref[sender(tp_ref[0], k, len(piece_refs))] = piece[...].astype(F32)
    rows = jnp.concatenate([order_ref[t] for t in range(len(piece_refs))], 1).astype(BF16)
    rows_ref[...] = rows
    gain = gain_ref[...]
    query = head_unit(project(rows, wq_ref), gain).astype(BF16)
    query_ref[...] = query
    groups, n_short, _ = send_ref.shape
    for g in range(groups):
        send_ref[g] = query[:n_short]
    query = query.astype(F32)
    new_key = head_unit(project(rows, wk_ref), gain).astype(BF16).astype(F32)
    new_value = project(rows, wv_ref).astype(BF16).astype(F32)
    own = [jnp.exp(c * math.sqrt(HEAD)) for c in head_cols(query * new_key)]
    den_ref[...] = spread_cols(own, query.shape)
    num_ref[...] = (
        spread_cols([o.astype(BF16).astype(F32) for o in own], query.shape) * new_value
    )


def den_tile(den, width):
    shape = (den.shape[0], width)
    high = den.astype(BF16).astype(F32)
    low = den - high
    lane, row = lanes(shape), rows_of(shape) % SUB
    return jnp.where(lane == row, high, jnp.where(lane == row + SUB, low, 0.0))


def cache_kernel(hit_ref, spread_ref, live_ref, q_ref, own_ref, lk_ref, lv_ref, k_ref, v_ref, out_ref, score_ref, num_ref, long_ref):
    slots, width, capacity = k_ref.shape
    groups, n_short, _ = q_ref.shape
    total = groups * n_short
    exp_rows = slots * SUB
    queries = q_ref[...].reshape(total, width)
    picked = jnp.dot(hit_ref[...], queries, preferred_element_type=F32)
    shape = (exp_rows, width)
    mask = (lanes(shape) // HEAD) == (rows_of(shape) % SUB)
    blocks = jnp.where(mask, picked * math.sqrt(HEAD), 0.0).astype(BF16)
    n_long = lk_ref.shape[0]
    long_query = own_ref[n_short : n_short + SUB].astype(F32) * math.sqrt(HEAD)
    mask8 = mask[:SUB]
    long_weights = []
    for i in range(n_long):
        row = jnp.broadcast_to(long_query[i : i + 1], mask8.shape)
        block = jnp.where(mask8, row, 0.0).astype(BF16)
        long_weights.append(jnp.exp(jnp.dot(block, lk_ref[i], preferred_element_type=F32)))
    for s in range(slots):
        at = slice(s * SUB, (s + 1) * SUB)
        score_ref[at] = jnp.dot(blocks[at], k_ref[s], preferred_element_type=F32)
    weights = jnp.where(live_ref[...] > 0.0, jnp.exp(score_ref[...]), 0.0)
    tail = out_ref.shape[-1] - width
    real = rows_of((exp_rows, tail)) % SUB < width // HEAD
    dens = den_tile(jnp.sum(weights, -1, keepdims=True), tail)
    dens = jnp.where(real, dens, 0.0).astype(BF16)
    spread = spread_ref[...]
    sent = jnp.dot(spread, dens, preferred_element_type=F32).astype(BF16)
    out_ref[:, :n_short, width:] = sent.reshape(groups, n_short, tail)
    long_ref[...] = jnp.zeros(long_ref.shape, F32)
    real8 = real[:SUB]
    for i in range(n_long):
        den = jnp.sum(long_weights[i], -1, keepdims=True)
        num = lax.dot_general(
            long_weights[i].astype(BF16), lv_ref[i], NT, preferred_element_type=F32
        )
        long_ref[i : i + 1, :width] = jnp.sum(jnp.where(mask8, num, 0.0), 0, keepdims=True)
        long_ref[i : i + 1, width:] = jnp.sum(
            jnp.where(real8, den_tile(den, tail), 0.0), 0, keepdims=True
        )
    extra = long_ref[...].astype(BF16)
    for g in range(groups):
        out_ref[g, n_short:, :] = extra
    top = rows_of((2 * SUB, capacity)) < SUB
    for s in range(0, slots, 2):
        at = slice(s * SUB, (s + 2) * SUB)
        pair = jnp.concatenate(
            [jnp.where(top, weights[at], 0.0), jnp.where(top, 0.0, weights[at])], 1
        )
        values = jnp.concatenate([v_ref[s], v_ref[s + 1]], 1)
        num_ref[at] = lax.dot_general(pair.astype(BF16), values, NT, preferred_element_type=F32)
    num = jnp.where(mask, num_ref[...], 0.0).astype(BF16)
    sent = jnp.dot(spread, num, preferred_element_type=F32).astype(BF16)
    out_ref[:, :n_short, :width] = sent.reshape(groups, n_short, width)


def combine_kernel(n_short, n_long, back_ref, den_ref, num_ref, w_ref, out_ref):
    width = num_ref.shape[-1]
    heads = width // HEAD
    total = back_ref[0].astype(F32)
    for g in range(1, back_ref.shape[0]):
        total = total + back_ref[g].astype(F32)
    dens = total[:, width:]
    cols = [dens[:, h : h + 1] + dens[:, SUB + h : SUB + h + 1] for h in range(heads)]
    den = den_ref[...] + spread_cols(cols, num_ref.shape)
    attended = ((total[:, :width] + num_ref[...]) / den).astype(BF16)
    proj = jnp.dot(attended, w_ref[...], preferred_element_type=F32)
    out_ref[...] = pack(proj, n_short, n_long).astype(BF16)


def pack(x, n_short, n_long):
    half, features = n_short // 2, x.shape[1]
    fold = half // n_long
    step = features // fold
    long_rows = x[n_short : n_short + n_long]
    folded = [long_rows[:, i * step : (i + 1) * step] for i in range(fold)]
    return jnp.concatenate([x[:half], x[half:n_short], jnp.concatenate(folded, 0)], 1)


def final_kernel(tp_ref, *refs):
    *part_refs, rows_ref, rate_ref, short_ref, long_ref = refs
    n_short, width = short_ref.shape
    n_long = long_ref.shape[0]
    features = rows_ref.shape[1]
    half = n_short // 2
    fold = half // n_long
    step = features // fold
    total = part_refs[0][...].astype(F32)
    for part in part_refs[1:]:
        total = total + part[...].astype(F32)
    short = jnp.concatenate([total[:, :features], total[:, features : 2 * features]], 0)
    folded = total[:, 2 * features :]
    long = jnp.concatenate([folded[i * n_long : (i + 1) * n_long] for i in range(fold)], 1)
    for proj, first, out_ref in ((short, 0, short_ref), (long, n_short, long_ref)):
        count = proj.shape[0]
        proj = proj * lax.rsqrt(jnp.sum(proj * proj, -1, keepdims=True) / features + EPS)
        state = rows_ref[...].astype(F32)[first : first + count]
        update = state + rate_ref[...] * (proj - state)
        square = jnp.sum(update * update, -1, keepdims=True)
        mine = update[:, :width]
        for t in range(1, features // width):
            mine = jnp.where(tp_ref[0] == t, update[:, t * width : (t + 1) * width], mine)
        out_ref[...] = (mine * lax.rsqrt(square / features + EPS)).astype(BF16)


def size_of(axis):
    return lax.axis_size(axis)


def from_all(x, axis):
    size = size_of(axis)
    got = []
    for k in range(size - 1, 0, -1):
        pairs = [(i, i ^ k if size & (size - 1) == 0 else (i + k) % size) for i in range(size)]
        got.append(lax.ppermute(x, axis, pairs))
    return [x, *got]


def exchange(x, axis):
    return lax.all_to_all(x, axis, split_axis=0, concat_axis=0, tiled=True)


VMEM = pl.BlockSpec(memory_space=pltpu.VMEM)
SMEM = pl.BlockSpec(memory_space=pltpu.SMEM)


def call(kernel, outs, ins, flops, moved, scratch=(), scalars=0, limit=16):
    return pl.pallas_call(
        kernel,
        out_shape=outs,
        in_specs=[SMEM] * scalars + [VMEM] * (len(ins) - scalars),
        out_specs=jax.tree.map(lambda _: VMEM, outs),
        scratch_shapes=scratch,
        compiler_params=pltpu.CompilerParams(vmem_limit_bytes=limit * 1024 * 1024),
        cost_estimate=pl.CostEstimate(flops=flops, bytes_accessed=moved, transcendentals=0),
    )(*ins)


def on_device(
    short_hidden,
    long_hidden,
    short_len,
    short_slot,
    w_query,
    w_key,
    w_value,
    w_out,
    qk_gain,
    step_rate,
    short_keys,
    short_values,
    long_keys,
    long_values,
):
    n_short, width = short_hidden.shape
    n_long = long_hidden.shape[0]
    groups = size_of("seq")
    features = w_query.shape[0]
    slots, capacity, _ = short_keys.shape
    total = short_len.shape[0]
    pad = -(n_short + n_long) % SUB
    count = n_short + n_long + pad
    sent_width = -(-(width + 2 * SUB) // 128) * 128
    out = jax.ShapeDtypeStruct
    tp_index = lax.axis_index("tp").reshape(1)
    base = (lax.axis_index("seq") * slots).reshape(1)

    mine = jnp.concatenate([short_hidden, long_hidden, jnp.zeros((pad, width), BF16)], 0)
    pieces = from_all(mine, "tp")
    w_query, w_key, w_value = w_query.T, w_key.T, w_value.T
    short_keys, short_values, long_keys, long_values = (
        jnp.swapaxes(a, 1, 2) for a in (short_keys, short_values, long_keys, long_values)
    )
    gain = call(gain_kernel, out((1, width), F32), (qk_gain.reshape(1, width),), 10**11, width)
    hit, spread, live, gain = call(
        prepare_kernel,
        (
            out((slots * SUB, total), BF16),
            out((total, slots * SUB), BF16),
            out((slots * SUB, capacity), F32),
            out((1, width), F32),
        ),
        (base, short_slot.reshape(1, total), short_len.reshape(1, total), gain),
        10**8,
        slots * SUB * total,
        scalars=1,
    )
    send, query, rows, own_den, own_num = call(
        query_kernel,
        (
            out((groups, n_short, width), BF16),
            out((count, width), BF16),
            out((count, features), BF16),
            out((count, width), F32),
            out((count, width), F32),
        ),
        (tp_index, *pieces, w_query, w_key, w_value, gain),
        10**11,
        6 * features * width,
        scratch=[pltpu.VMEM((len(pieces), count, width), F32)],
        scalars=1,
    )
    queries = exchange(send, "seq")
    sent = call(
        cache_kernel,
        out((groups, count, sent_width), BF16),
        (hit, spread, live, queries, query, long_keys, long_values, short_keys, short_values),
        10**8,
        4 * short_keys.size + 4 * long_keys.size,
        scratch=[
            pltpu.VMEM((slots * SUB, capacity), F32),
            pltpu.VMEM((slots * SUB, width), F32),
            pltpu.VMEM((count - n_short, sent_width), F32),
        ],
    )
    back = exchange(sent, "seq")
    partial = call(
        functools.partial(combine_kernel, n_short, n_long),
        out((n_short // 2, 2 * features + 2 * n_long * features // n_short), BF16),
        (back, own_den, own_num, w_out),
        2 * count * features * width,
        2 * features * width,
    )
    partials = from_all(partial, "tp")
    return call(
        final_kernel,
        (out((n_short, width), BF16), out((n_long, width), BF16)),
        (tp_index, *partials, rows, step_rate.reshape(1, features)),
        10 * count * features,
        10 * count * features,
        scalars=1,
    )


def solution(mesh):
    return jax.shard_map(
        on_device,
        mesh=mesh,
        in_specs=(
            P("seq", "tp"),
            P(None, "tp"),
            P(),
            P(),
            P(None, "tp"),
            P(None, "tp"),
            P(None, "tp"),
            P("tp", None),
            P("tp"),
            P(),
            P("seq", None, "tp"),
            P("seq", None, "tp"),
            P(None, "seq", "tp"),
            P(None, "seq", "tp"),
        ),
        out_specs=(P("seq", "tp"), P(None, "tp")),
        check_vma=False,
    )
```

```python
import functools
import math

import jax
import jax.numpy as jnp
from jax import lax
from jax.experimental import pallas as pl
from jax.experimental.pallas import tpu as pltpu
from jax.sharding import PartitionSpec as P

HEAD = 64
EPS = 1e-06
SUB = 8
BF16 = jnp.bfloat16
F32 = jnp.float32
NT = (((1,), (1,)), ((), ()))


def lanes(shape):
    return lax.broadcasted_iota(jnp.int32, shape, len(shape) - 1)


def rows_of(shape):
    return lax.broadcasted_iota(jnp.int32, shape, len(shape) - 2)


def head_cols(x):
    head = lanes(x.shape) // HEAD
    return [
        jnp.sum(jnp.where(head == h, x, 0.0), -1, keepdims=True)
        for h in range(x.shape[-1] // HEAD)
    ]


def spread_cols(cols, shape):
    head = lanes(shape) // HEAD
    out = jnp.broadcast_to(cols[0], shape)
    for h in range(1, len(cols)):
        out = jnp.where(head == h, cols[h], out)
    return out


def head_unit(x, gain):
    scale = spread_cols([lax.rsqrt(c + EPS) for c in head_cols(x * x)], x.shape)
    return x * scale * gain


def project(rows, w_ref):
    return lax.dot_general(rows, w_ref[...], NT, preferred_element_type=F32)


def join_kernel(short_hbm, long_hbm, out_ref, short_ref, long_ref, sems):
    first = pltpu.make_async_copy(short_hbm, short_ref, sems.at[0])
    second = pltpu.make_async_copy(long_hbm, long_ref, sems.at[1])
    first.start()
    second.start()
    first.wait()
    second.wait()
    n_short, n_long = short_ref.shape[0], long_ref.shape[0]
    out_ref[:n_short] = short_ref[...]
    pad = out_ref.shape[0] - n_short - n_long
    rest = [long_ref[...].astype(F32), jnp.zeros((pad, out_ref.shape[1]), F32)]
    out_ref[n_short:] = jnp.concatenate(rest, 0).astype(BF16)


def gain_kernel(gain_ref, row_ref):
    row_ref[...] = gain_ref[...]


def prepare_kernel(base_ref, slot_ref, len_ref, gain_ref, hit_ref, spread_ref, live_ref, row_ref):
    row_ref[...] = gain_ref[...]
    exp_rows, total = hit_ref.shape
    hit = slot_ref[...] - base_ref[0] == rows_of((exp_rows, total)) // SUB
    ones = jnp.where(hit, 1.0, 0.0)
    hit_ref[...] = ones.astype(BF16)
    spread_ref[...] = ones.T.astype(BF16)
    lengths = jnp.sum(jnp.where(hit, len_ref[...], 0), -1, keepdims=True)
    live_ref[...] = jnp.where(lanes(live_ref.shape) < lengths, 1.0, 0.0)


def sender(me, place, size):
    k = (size - place) % size
    return me ^ k if size & (size - 1) == 0 else lax.rem(me - k + size, size)


def query_kernel(tp_ref, *refs):
    *piece_refs, wq_ref, gain_ref, send_ref, query_ref, rows_ref, order_ref = refs
    for k, piece in enumerate(piece_refs):
        order_ref[sender(tp_ref[0], k, len(piece_refs))] = piece[...].astype(F32)
    rows = jnp.concatenate([order_ref[t] for t in range(len(piece_refs))], 1).astype(BF16)
    rows_ref[...] = rows
    gain = gain_ref[...]
    query = head_unit(project(rows, wq_ref), gain).astype(BF16)
    query_ref[...] = query
    groups, n_short, _ = send_ref.shape
    for g in range(groups):
        send_ref[g] = query[:n_short]


def den_tile(den, width):
    shape = (den.shape[0], width)
    high = den.astype(BF16).astype(F32)
    low = den - high
    lane, row = lanes(shape), rows_of(shape) % SUB
    return jnp.where(lane == row, high, jnp.where(lane == row + SUB, low, 0.0))


def own_terms(rows, query, wk_ref, wv_ref, gain):
    new_key = head_unit(project(rows, wk_ref), gain).astype(BF16).astype(F32)
    new_value = project(rows, wv_ref).astype(BF16).astype(F32)
    own = [jnp.exp(c * math.sqrt(HEAD)) for c in head_cols(query * new_key)]
    rounded = [o.astype(BF16).astype(F32) for o in own]
    return spread_cols(own, query.shape), spread_cols(rounded, query.shape) * new_value


def cache_kernel(hit_ref, spread_ref, live_ref, q_ref, own_ref, rows_ref, wk_ref, wv_ref, gain_ref, lk_ref, lv_ref, k_ref, v_ref, out_ref, own_den_ref, own_num_ref, score_ref, num_ref, long_ref):
    own_den_ref[...], own_num_ref[...] = own_terms(
        rows_ref[...], own_ref[...].astype(F32), wk_ref, wv_ref, gain_ref[...]
    )
    slots, width, capacity = k_ref.shape
    groups, n_short, _ = q_ref.shape
    total = groups * n_short
    exp_rows = slots * SUB
    queries = q_ref[...].reshape(total, width)
    picked = jnp.dot(hit_ref[...], queries, preferred_element_type=F32)
    shape = (exp_rows, width)
    mask = (lanes(shape) // HEAD) == (rows_of(shape) % SUB)
    blocks = jnp.where(mask, picked * math.sqrt(HEAD), 0.0).astype(BF16)
    n_long = lk_ref.shape[0]
    long_query = own_ref[n_short : n_short + SUB].astype(F32) * math.sqrt(HEAD)
    mask8 = mask[:SUB]
    long_weights = []
    for i in range(n_long):
        row = jnp.broadcast_to(long_query[i : i + 1], mask8.shape)
        block = jnp.where(mask8, row, 0.0).astype(BF16)
        long_weights.append(jnp.exp(jnp.dot(block, lk_ref[i], preferred_element_type=F32)))
    for s in range(0, slots, 2):
        keys = jnp.concatenate([k_ref[s], k_ref[s + 1]], 1)
        both = jnp.dot(blocks[s * SUB : (s + 2) * SUB], keys, preferred_element_type=F32)
        score_ref[s * SUB : (s + 1) * SUB] = both[:SUB, :capacity]
        score_ref[(s + 1) * SUB : (s + 2) * SUB] = both[SUB:, capacity:]
    weights = jnp.where(live_ref[...] > 0.0, jnp.exp(score_ref[...]), 0.0)
    tail = out_ref.shape[-1] - width
    real = rows_of((exp_rows, tail)) % SUB < width // HEAD
    dens = den_tile(jnp.sum(weights, -1, keepdims=True), tail)
    dens = jnp.where(real, dens, 0.0).astype(BF16)
    spread = spread_ref[...]
    long_ref[...] = jnp.zeros(long_ref.shape, F32)
    real8 = real[:SUB]
    for i in range(n_long):
        den = jnp.sum(long_weights[i], -1, keepdims=True)
        num = lax.dot_general(
            long_weights[i].astype(BF16), lv_ref[i], NT, preferred_element_type=F32
        )
        long_ref[i : i + 1, :width] = jnp.sum(jnp.where(mask8, num, 0.0), 0, keepdims=True)
        long_ref[i : i + 1, width:] = jnp.sum(
            jnp.where(real8, den_tile(den, tail), 0.0), 0, keepdims=True
        )
    extra = long_ref[...].astype(BF16)
    for g in range(groups):
        out_ref[g, n_short:, :] = extra
    top = rows_of((2 * SUB, capacity)) < SUB
    for s in range(0, slots, 2):
        at = slice(s * SUB, (s + 2) * SUB)
        pair = jnp.concatenate(
            [jnp.where(top, weights[at], 0.0), jnp.where(top, 0.0, weights[at])], 1
        )
        values = jnp.concatenate([v_ref[s], v_ref[s + 1]], 1)
        num_ref[at] = lax.dot_general(pair.astype(BF16), values, NT, preferred_element_type=F32)
    num = jnp.where(mask, num_ref[...], 0.0).astype(BF16)
    sent = jnp.dot(spread, jnp.concatenate([num, dens], 1), preferred_element_type=F32)
    out_ref[:, :n_short, :] = sent.astype(BF16).reshape(groups, n_short, width + tail)


def combine_kernel(n_short, n_long, back_ref, den_ref, num_ref, w_ref, out_ref):
    width = num_ref.shape[-1]
    heads = width // HEAD
    total = back_ref[0].astype(F32)
    for g in range(1, back_ref.shape[0]):
        total = total + back_ref[g].astype(F32)
    dens = total[:, width:]
    cols = [dens[:, h : h + 1] + dens[:, SUB + h : SUB + h + 1] for h in range(heads)]
    den = den_ref[...] + spread_cols(cols, num_ref.shape)
    attended = ((total[:, :width] + num_ref[...]) / den).astype(BF16)
    proj = jnp.dot(attended, w_ref[...], preferred_element_type=F32)
    out_ref[...] = pack(proj, n_short, n_long).astype(BF16)


def pack(x, n_short, n_long):
    half, features = n_short // 2, x.shape[1]
    fold = half // n_long
    step = features // fold
    long_rows = x[n_short : n_short + n_long]
    folded = [long_rows[:, i * step : (i + 1) * step] for i in range(fold)]
    return jnp.concatenate([x[:half], x[half:n_short], jnp.concatenate(folded, 0)], 1)


def final_kernel(tp_ref, *refs):
    *part_refs, rows_ref, rate_ref, short_ref, long_ref = refs
    n_short, width = short_ref.shape
    n_long = long_ref.shape[0]
    features = rows_ref.shape[1]
    half = n_short // 2
    fold = half // n_long
    step = features // fold
    total = part_refs[0][...].astype(F32)
    for part in part_refs[1:]:
        total = total + part[...].astype(F32)
    short = jnp.concatenate([total[:, :features], total[:, features : 2 * features]], 0)
    folded = total[:, 2 * features :]
    long = jnp.concatenate([folded[i * n_long : (i + 1) * n_long] for i in range(fold)], 1)
    for proj, first, out_ref in ((short, 0, short_ref), (long, n_short, long_ref)):
        count = proj.shape[0]
        proj = proj * lax.rsqrt(jnp.sum(proj * proj, -1, keepdims=True) / features + EPS)
        state = rows_ref[...].astype(F32)[first : first + count]
        update = state + rate_ref[...] * (proj - state)
        square = jnp.sum(update * update, -1, keepdims=True)
        mine = update[:, :width]
        for t in range(1, features // width):
            mine = jnp.where(tp_ref[0] == t, update[:, t * width : (t + 1) * width], mine)
        out_ref[...] = (mine * lax.rsqrt(square / features + EPS)).astype(BF16)


def size_of(axis):
    return lax.axis_size(axis)


def from_all(x, axis):
    size = size_of(axis)
    got = []
    for k in range(size - 1, 0, -1):
        pairs = [(i, i ^ k if size & (size - 1) == 0 else (i + k) % size) for i in range(size)]
        got.append(lax.ppermute(x, axis, pairs))
    return [x, *got]


def exchange(x, axis):
    return lax.all_to_all(x, axis, split_axis=0, concat_axis=0, tiled=True)


VMEM = pl.BlockSpec(memory_space=pltpu.VMEM)
DISTANT = pl.BlockSpec(memory_space=pltpu.HBM)
SMEM = pl.BlockSpec(memory_space=pltpu.SMEM)


def call(kernel, outs, ins, flops, moved, scratch=(), scalars=0, limit=16, distant=0):
    return pl.pallas_call(
        kernel,
        out_shape=outs,
        in_specs=[SMEM] * scalars + [VMEM] * (len(ins) - scalars - distant) + [DISTANT] * distant,
        out_specs=jax.tree.map(lambda _: VMEM, outs),
        scratch_shapes=scratch,
        compiler_params=pltpu.CompilerParams(vmem_limit_bytes=limit * 1024 * 1024),
        cost_estimate=pl.CostEstimate(flops=flops, bytes_accessed=moved, transcendentals=0),
    )(*ins)


def on_device(
    short_hidden,
    long_hidden,
    short_len,
    short_slot,
    w_query,
    w_key,
    w_value,
    w_out,
    qk_gain,
    step_rate,
    short_keys,
    short_values,
    long_keys,
    long_values,
):
    n_short, width = short_hidden.shape
    n_long = long_hidden.shape[0]
    groups = size_of("seq")
    features = w_query.shape[0]
    slots, capacity, _ = short_keys.shape
    total = short_len.shape[0]
    pad = -(n_short + n_long) % SUB
    count = n_short + n_long + pad
    sent_width = -(-(width + 2 * SUB) // 128) * 128
    out = jax.ShapeDtypeStruct
    tp_index = lax.axis_index("tp").reshape(1)
    base = (lax.axis_index("seq") * slots).reshape(1)

    mine = call(
        join_kernel,
        out((count, width), BF16),
        tuple(pltpu.with_memory_space_constraint(a, pltpu.HBM) for a in (short_hidden, long_hidden)),
        0,
        4 * count * width,
        scratch=[
            pltpu.VMEM(short_hidden.shape, BF16),
            pltpu.VMEM(long_hidden.shape, BF16),
            pltpu.SemaphoreType.DMA((2,)),
        ],
        distant=2,
    )
    pieces = from_all(mine, "tp")
    w_query, w_key, w_value = w_query.T, w_key.T, w_value.T
    short_keys, short_values, long_keys, long_values = (
        jnp.swapaxes(a, 1, 2) for a in (short_keys, short_values, long_keys, long_values)
    )
    gain = call(gain_kernel, out((1, width), F32), (qk_gain.reshape(1, width),), 10**11, width)
    hit, spread, live, gain = call(
        prepare_kernel,
        (
            out((slots * SUB, total), BF16),
            out((total, slots * SUB), BF16),
            out((slots * SUB, capacity), F32),
            out((1, width), F32),
        ),
        (base, short_slot.reshape(1, total), short_len.reshape(1, total), gain),
        10**8,
        slots * SUB * total,
        scalars=1,
    )
    send, query, rows = call(
        query_kernel,
        (
            out((groups, n_short, width), BF16),
            out((count, width), BF16),
            out((count, features), BF16),
        ),
        (tp_index, *pieces, w_query, gain),
        10**11,
        6 * features * width,
        scratch=[pltpu.VMEM((len(pieces), count, width), F32)],
        scalars=1,
    )
    queries = exchange(send, "seq")
    sent, own_den, own_num = call(
        cache_kernel,
        (
            out((groups, count, sent_width), BF16),
            out((count, width), F32),
            out((count, width), F32),
        ),
        (hit, spread, live, queries, query, rows, w_key, w_value, gain, long_keys, long_values, short_keys, short_values),
        10**8,
        4 * short_keys.size + 4 * long_keys.size,
        scratch=[
            pltpu.VMEM((slots * SUB, capacity), F32),
            pltpu.VMEM((slots * SUB, width), F32),
            pltpu.VMEM((count - n_short, sent_width), F32),
        ],
    )
    back = exchange(sent, "seq")
    partial = call(
        functools.partial(combine_kernel, n_short, n_long),
        out((n_short // 2, 2 * features + 2 * n_long * features // n_short), BF16),
        (back, own_den, own_num, w_out),
        2 * count * features * width,
        2 * features * width,
    )
    partials = from_all(partial, "tp")
    return call(
        final_kernel,
        (out((n_short, width), BF16), out((n_long, width), BF16)),
        (tp_index, *partials, rows, step_rate.reshape(1, features)),
        10 * count * features,
        10 * count * features,
        scalars=1,
    )


def solution(mesh):
    return jax.shard_map(
        on_device,
        mesh=mesh,
        in_specs=(
            P("seq", "tp"),
            P(None, "tp"),
            P(),
            P(),
            P(None, "tp"),
            P(None, "tp"),
            P(None, "tp"),
            P("tp", None),
            P("tp"),
            P(),
            P("seq", None, "tp"),
            P("seq", None, "tp"),
            P(None, "seq", "tp"),
            P(None, "seq", "tp"),
        ),
        out_specs=(P("seq", "tp"), P(None, "tp")),
        check_vma=False,
    )
```

```python
import functools
import math

import jax
import jax.numpy as jnp
from jax import lax
from jax.experimental import pallas as pl
from jax.experimental.pallas import tpu as pltpu
from jax.sharding import PartitionSpec as P

HEAD = 64
EPS = 1e-06
SUB = 8
BF16 = jnp.bfloat16
F32 = jnp.float32
NT = (((1,), (1,)), ((), ()))


def lanes(shape):
    return lax.broadcasted_iota(jnp.int32, shape, len(shape) - 1)


def rows_of(shape):
    return lax.broadcasted_iota(jnp.int32, shape, len(shape) - 2)


def head_cols(x):
    head = lanes(x.shape) // HEAD
    return [
        jnp.sum(jnp.where(head == h, x, 0.0), -1, keepdims=True)
        for h in range(x.shape[-1] // HEAD)
    ]


def spread_cols(cols, shape):
    head = lanes(shape) // HEAD
    out = jnp.broadcast_to(cols[0], shape)
    for h in range(1, len(cols)):
        out = jnp.where(head == h, cols[h], out)
    return out


def head_unit(x, gain):
    scale = spread_cols([lax.rsqrt(c + EPS) for c in head_cols(x * x)], x.shape)
    return x * scale * gain


def project(rows, w_ref):
    return lax.dot_general(rows, w_ref[...], NT, preferred_element_type=F32)


def join_kernel(short_hbm, long_hbm, out_ref, short_ref, long_ref, sems):
    first = pltpu.make_async_copy(short_hbm, short_ref, sems.at[0])
    second = pltpu.make_async_copy(long_hbm, long_ref, sems.at[1])
    first.start()
    second.start()
    first.wait()
    second.wait()
    n_short, n_long = short_ref.shape[0], long_ref.shape[0]
    out_ref[:n_short] = short_ref[...]
    pad = out_ref.shape[0] - n_short - n_long
    rest = [long_ref[...].astype(F32), jnp.zeros((pad, out_ref.shape[1]), F32)]
    out_ref[n_short:] = jnp.concatenate(rest, 0).astype(BF16)


def gain_kernel(gain_ref, row_ref):
    row_ref[...] = gain_ref[...]


def prepare_kernel(base_ref, slot_ref, len_ref, gain_ref, hit_ref, spread_ref, live_ref, row_ref):
    row_ref[...] = gain_ref[...]
    exp_rows, total = hit_ref.shape
    hit = slot_ref[...] - base_ref[0] == rows_of((exp_rows, total)) // SUB
    ones = jnp.where(hit, 1.0, 0.0)
    hit_ref[...] = ones.astype(BF16)
    spread_ref[...] = ones.T.astype(BF16)
    lengths = jnp.sum(jnp.where(hit, len_ref[...], 0), -1, keepdims=True)
    live_ref[...] = jnp.where(lanes(live_ref.shape) < lengths, 1.0, 0.0)


def sender(me, place, size):
    k = (size - place) % size
    return me ^ k if size & (size - 1) == 0 else lax.rem(me - k + size, size)


def query_kernel(tp_ref, *refs):
    *piece_refs, wq_ref, gain_ref, send_ref, query_ref, rows_ref, order_ref = refs
    for k, piece in enumerate(piece_refs):
        order_ref[sender(tp_ref[0], k, len(piece_refs))] = piece[...].astype(F32)
    rows = jnp.concatenate([order_ref[t] for t in range(len(piece_refs))], 1).astype(BF16)
    rows_ref[...] = rows
    gain = gain_ref[...]
    query = head_unit(project(rows, wq_ref), gain).astype(BF16)
    query_ref[...] = query
    groups, n_short, _ = send_ref.shape
    for g in range(groups):
        send_ref[g] = query[:n_short]


def den_tile(den, width):
    shape = (den.shape[0], width)
    high = den.astype(BF16).astype(F32)
    low = den - high
    lane, row = lanes(shape), rows_of(shape) % SUB
    return jnp.where(lane == row, high, jnp.where(lane == row + SUB, low, 0.0))


def own_terms(rows, query, wk_ref, wv_ref, gain):
    new_key = head_unit(project(rows, wk_ref), gain).astype(BF16).astype(F32)
    new_value = project(rows, wv_ref).astype(BF16).astype(F32)
    own = [jnp.exp(c * math.sqrt(HEAD)) for c in head_cols(query * new_key)]
    rounded = [o.astype(BF16).astype(F32) for o in own]
    return spread_cols(own, query.shape), spread_cols(rounded, query.shape) * new_value


def cache_kernel(hit_ref, spread_ref, live_ref, q_ref, own_ref, rows_ref, wk_ref, wv_ref, gain_ref, lk_ref, lv_ref, k_ref, v_ref, out_ref, own_den_ref, own_num_ref, score_ref, num_ref, long_ref):
    own_den_ref[...], own_num_ref[...] = own_terms(
        rows_ref[...], own_ref[...].astype(F32), wk_ref, wv_ref, gain_ref[...]
    )
    slots, width, capacity = k_ref.shape
    groups, n_short, _ = q_ref.shape
    total = groups * n_short
    exp_rows = slots * SUB
    queries = q_ref[...].reshape(total, width)
    picked = jnp.dot(hit_ref[...], queries, preferred_element_type=F32)
    shape = (exp_rows, width)
    mask = (lanes(shape) // HEAD) == (rows_of(shape) % SUB)
    blocks = jnp.where(mask, picked * math.sqrt(HEAD), 0.0).astype(BF16)
    n_long = lk_ref.shape[0]
    long_query = own_ref[n_short : n_short + SUB].astype(F32) * math.sqrt(HEAD)
    mask8 = mask[:SUB]
    long_weights = []
    for i in range(n_long):
        row = jnp.broadcast_to(long_query[i : i + 1], mask8.shape)
        block = jnp.where(mask8, row, 0.0).astype(BF16)
        long_weights.append(jnp.exp(jnp.dot(block, lk_ref[i], preferred_element_type=F32)))
    for s in range(0, slots, 2):
        keys = jnp.concatenate([k_ref[s], k_ref[s + 1]], 1)
        both = jnp.dot(blocks[s * SUB : (s + 2) * SUB], keys, preferred_element_type=F32)
        score_ref[s * SUB : (s + 1) * SUB] = both[:SUB, :capacity]
        score_ref[(s + 1) * SUB : (s + 2) * SUB] = both[SUB:, capacity:]
    weights = jnp.where(live_ref[...] > 0.0, jnp.exp(score_ref[...]), 0.0)
    tail = out_ref.shape[-1] - width
    real = rows_of((exp_rows, tail)) % SUB < width // HEAD
    dens = den_tile(jnp.sum(weights, -1, keepdims=True), tail)
    dens = jnp.where(real, dens, 0.0).astype(BF16)
    spread = spread_ref[...]
    top = rows_of((2 * SUB, capacity)) < SUB
    for s in range(0, slots, 2):
        at = slice(s * SUB, (s + 2) * SUB)
        pair = jnp.concatenate(
            [jnp.where(top, weights[at], 0.0), jnp.where(top, 0.0, weights[at])], 1
        )
        values = jnp.concatenate([v_ref[s], v_ref[s + 1]], 1)
        num_ref[at] = lax.dot_general(pair.astype(BF16), values, NT, preferred_element_type=F32)
    long_ref[...] = jnp.zeros(long_ref.shape, F32)
    real8 = real[:SUB]
    for i in range(n_long):
        den = jnp.sum(long_weights[i], -1, keepdims=True)
        num = lax.dot_general(
            long_weights[i].astype(BF16), lv_ref[i], NT, preferred_element_type=F32
        )
        long_ref[i : i + 1, :width] = jnp.sum(jnp.where(mask8, num, 0.0), 0, keepdims=True)
        long_ref[i : i + 1, width:] = jnp.sum(
            jnp.where(real8, den_tile(den, tail), 0.0), 0, keepdims=True
        )
    extra = long_ref[...].astype(BF16)
    for g in range(groups):
        out_ref[g, n_short:, :] = extra
    num = jnp.where(mask, num_ref[...], 0.0).astype(BF16)
    sent = jnp.dot(spread, jnp.concatenate([num, dens], 1), preferred_element_type=F32)
    out_ref[:, :n_short, :] = sent.astype(BF16).reshape(groups, n_short, width + tail)


def combine_kernel(n_short, n_long, back_ref, den_ref, num_ref, w_ref, out_ref):
    width = num_ref.shape[-1]
    heads = width // HEAD
    total = back_ref[0].astype(F32)
    for g in range(1, back_ref.shape[0]):
        total = total + back_ref[g].astype(F32)
    dens = total[:, width:]
    cols = [dens[:, h : h + 1] + dens[:, SUB + h : SUB + h + 1] for h in range(heads)]
    den = den_ref[...] + spread_cols(cols, num_ref.shape)
    attended = ((total[:, :width] + num_ref[...]) / den).astype(BF16)
    proj = jnp.dot(attended, w_ref[...], preferred_element_type=F32)
    out_ref[...] = pack(proj, n_short, n_long).astype(BF16)


def pack(x, n_short, n_long):
    half, features = n_short // 2, x.shape[1]
    fold = half // n_long
    step = features // fold
    long_rows = x[n_short : n_short + n_long]
    folded = [long_rows[:, i * step : (i + 1) * step] for i in range(fold)]
    return jnp.concatenate([x[:half], x[half:n_short], jnp.concatenate(folded, 0)], 1)


def final_kernel(tp_ref, *refs):
    *part_refs, rows_ref, rate_ref, short_ref, long_ref = refs
    n_short, width = short_ref.shape
    n_long = long_ref.shape[0]
    features = rows_ref.shape[1]
    half = n_short // 2
    fold = half // n_long
    step = features // fold
    total = part_refs[0][...].astype(F32)
    for part in part_refs[1:]:
        total = total + part[...].astype(F32)
    short = jnp.concatenate([total[:, :features], total[:, features : 2 * features]], 0)
    folded = total[:, 2 * features :]
    long = jnp.concatenate([folded[i * n_long : (i + 1) * n_long] for i in range(fold)], 1)
    for proj, first, out_ref in ((short, 0, short_ref), (long, n_short, long_ref)):
        count = proj.shape[0]
        proj = proj * lax.rsqrt(jnp.sum(proj * proj, -1, keepdims=True) / features + EPS)
        state = rows_ref[...].astype(F32)[first : first + count]
        update = state + rate_ref[...] * (proj - state)
        square = jnp.sum(update * update, -1, keepdims=True)
        mine = update[:, :width]
        for t in range(1, features // width):
            mine = jnp.where(tp_ref[0] == t, update[:, t * width : (t + 1) * width], mine)
        out_ref[...] = (mine * lax.rsqrt(square / features + EPS)).astype(BF16)


def size_of(axis):
    return lax.axis_size(axis)


def from_all(x, axis):
    size = size_of(axis)
    got = []
    for k in range(size - 1, 0, -1):
        pairs = [(i, i ^ k if size & (size - 1) == 0 else (i + k) % size) for i in range(size)]
        got.append(lax.ppermute(x, axis, pairs))
    return [x, *got]


def exchange(x, axis):
    return lax.all_to_all(x, axis, split_axis=0, concat_axis=0, tiled=True)


VMEM = pl.BlockSpec(memory_space=pltpu.VMEM)
DISTANT = pl.BlockSpec(memory_space=pltpu.HBM)
SMEM = pl.BlockSpec(memory_space=pltpu.SMEM)


def call(kernel, outs, ins, flops, moved, scratch=(), scalars=0, limit=16, distant=0):
    return pl.pallas_call(
        kernel,
        out_shape=outs,
        in_specs=[SMEM] * scalars + [VMEM] * (len(ins) - scalars - distant) + [DISTANT] * distant,
        out_specs=jax.tree.map(lambda _: VMEM, outs),
        scratch_shapes=scratch,
        compiler_params=pltpu.CompilerParams(vmem_limit_bytes=limit * 1024 * 1024),
        cost_estimate=pl.CostEstimate(flops=flops, bytes_accessed=moved, transcendentals=0),
    )(*ins)


def on_device(
    short_hidden,
    long_hidden,
    short_len,
    short_slot,
    w_query,
    w_key,
    w_value,
    w_out,
    qk_gain,
    step_rate,
    short_keys,
    short_values,
    long_keys,
    long_values,
):
    n_short, width = short_hidden.shape
    n_long = long_hidden.shape[0]
    groups = size_of("seq")
    features = w_query.shape[0]
    slots, capacity, _ = short_keys.shape
    total = short_len.shape[0]
    pad = -(n_short + n_long) % SUB
    count = n_short + n_long + pad
    sent_width = -(-(width + 2 * SUB) // 128) * 128
    out = jax.ShapeDtypeStruct
    tp_index = lax.axis_index("tp").reshape(1)
    base = (lax.axis_index("seq") * slots).reshape(1)

    mine = call(
        join_kernel,
        out((count, width), BF16),
        tuple(pltpu.with_memory_space_constraint(a, pltpu.HBM) for a in (short_hidden, long_hidden)),
        0,
        4 * count * width,
        scratch=[
            pltpu.VMEM(short_hidden.shape, BF16),
            pltpu.VMEM(long_hidden.shape, BF16),
            pltpu.SemaphoreType.DMA((2,)),
        ],
        distant=2,
    )
    pieces = from_all(mine, "tp")
    w_query, w_key, w_value = w_query.T, w_key.T, w_value.T
    short_keys, short_values, long_keys, long_values = (
        jnp.swapaxes(a, 1, 2) for a in (short_keys, short_values, long_keys, long_values)
    )
    gain = call(gain_kernel, out((1, width), F32), (qk_gain.reshape(1, width),), 10**11, width)
    hit, spread, live, gain = call(
        prepare_kernel,
        (
            out((slots * SUB, total), BF16),
            out((total, slots * SUB), BF16),
            out((slots * SUB, capacity), F32),
            out((1, width), F32),
        ),
        (base, short_slot.reshape(1, total), short_len.reshape(1, total), gain),
        10**8,
        slots * SUB * total,
        scalars=1,
    )
    send, query, rows = call(
        query_kernel,
        (
            out((groups, n_short, width), BF16),
            out((count, width), BF16),
            out((count, features), BF16),
        ),
        (tp_index, *pieces, w_query, gain),
        10**11,
        6 * features * width,
        scratch=[pltpu.VMEM((len(pieces), count, width), F32)],
        scalars=1,
    )
    queries = exchange(send, "seq")
    sent, own_den, own_num = call(
        cache_kernel,
        (
            out((groups, count, sent_width), BF16),
            out((count, width), F32),
            out((count, width), F32),
        ),
        (hit, spread, live, queries, query, rows, w_key, w_value, gain, long_keys, long_values, short_keys, short_values),
        10**8,
        4 * short_keys.size + 4 * long_keys.size,
        scratch=[
            pltpu.VMEM((slots * SUB, capacity), F32),
            pltpu.VMEM((slots * SUB, width), F32),
            pltpu.VMEM((count - n_short, sent_width), F32),
        ],
    )
    back = exchange(sent, "seq")
    partial = call(
        functools.partial(combine_kernel, n_short, n_long),
        out((n_short // 2, 2 * features + 2 * n_long * features // n_short), BF16),
        (back, own_den, own_num, w_out),
        2 * count * features * width,
        2 * features * width,
    )
    partials = from_all(partial, "tp")
    return call(
        final_kernel,
        (out((n_short, width), BF16), out((n_long, width), BF16)),
        (tp_index, *partials, rows, step_rate.reshape(1, features)),
        10 * count * features,
        10 * count * features,
        scalars=1,
    )


def solution(mesh):
    return jax.shard_map(
        on_device,
        mesh=mesh,
        in_specs=(
            P("seq", "tp"),
            P(None, "tp"),
            P(),
            P(),
            P(None, "tp"),
            P(None, "tp"),
            P(None, "tp"),
            P("tp", None),
            P("tp"),
            P(),
            P("seq", None, "tp"),
            P("seq", None, "tp"),
            P(None, "seq", "tp"),
            P(None, "seq", "tp"),
        ),
        out_specs=(P("seq", "tp"), P(None, "tp")),
        check_vma=False,
    )
```

```python
import functools
import math

import jax
import jax.numpy as jnp
from jax import lax
from jax.experimental import pallas as pl
from jax.experimental.pallas import tpu as pltpu
from jax.sharding import PartitionSpec as P

HEAD = 64
EPS = 1e-06
SUB = 8
BF16 = jnp.bfloat16
F32 = jnp.float32
NT = (((1,), (1,)), ((), ()))


def lanes(shape):
    return lax.broadcasted_iota(jnp.int32, shape, len(shape) - 1)


def rows_of(shape):
    return lax.broadcasted_iota(jnp.int32, shape, len(shape) - 2)


def head_cols(x):
    head = lanes(x.shape) // HEAD
    return [
        jnp.sum(jnp.where(head == h, x, 0.0), -1, keepdims=True)
        for h in range(x.shape[-1] // HEAD)
    ]


def spread_cols(cols, shape):
    head = lanes(shape) // HEAD
    out = jnp.broadcast_to(cols[0], shape)
    for h in range(1, len(cols)):
        out = jnp.where(head == h, cols[h], out)
    return out


def head_unit(x, gain):
    scale = spread_cols([lax.rsqrt(c + EPS) for c in head_cols(x * x)], x.shape)
    return x * scale * gain


def project(rows, w_ref):
    return lax.dot_general(rows, w_ref[...], NT, preferred_element_type=F32)


def join_kernel(short_hbm, long_hbm, out_ref, short_ref, long_ref, sems):
    first = pltpu.make_async_copy(short_hbm, short_ref, sems.at[0])
    second = pltpu.make_async_copy(long_hbm, long_ref, sems.at[1])
    first.start()
    second.start()
    first.wait()
    second.wait()
    n_short, n_long = short_ref.shape[0], long_ref.shape[0]
    out_ref[:n_short] = short_ref[...]
    pad = out_ref.shape[0] - n_short - n_long
    rest = [long_ref[...].astype(F32), jnp.zeros((pad, out_ref.shape[1]), F32)]
    out_ref[n_short:] = jnp.concatenate(rest, 0).astype(BF16)


def gain_kernel(gain_ref, row_ref):
    row_ref[...] = gain_ref[...]


def prepare_kernel(base_ref, slot_ref, len_ref, gain_ref, hit_ref, spread_ref, live_ref, row_ref):
    row_ref[...] = gain_ref[...]
    exp_rows, total = hit_ref.shape
    hit = slot_ref[...] - base_ref[0] == rows_of((exp_rows, total)) // SUB
    ones = jnp.where(hit, 1.0, 0.0)
    hit_ref[...] = ones.astype(BF16)
    spread_ref[...] = ones.T.astype(BF16)
    lengths = jnp.sum(jnp.where(hit, len_ref[...], 0), -1, keepdims=True)
    live_ref[...] = jnp.where(lanes(live_ref.shape) < lengths, 1.0, 0.0)


def sender(me, place, size):
    k = (size - place) % size
    return me ^ k if size & (size - 1) == 0 else lax.rem(me - k + size, size)


def query_kernel(tp_ref, *refs):
    *piece_refs, wq_ref, gain_ref, send_ref, query_ref, rows_ref, order_ref = refs
    for k, piece in enumerate(piece_refs):
        order_ref[sender(tp_ref[0], k, len(piece_refs))] = piece[...].astype(F32)
    rows = jnp.concatenate([order_ref[t] for t in range(len(piece_refs))], 1).astype(BF16)
    rows_ref[...] = rows
    gain = gain_ref[...]
    query = head_unit(project(rows, wq_ref), gain).astype(BF16)
    query_ref[...] = query
    groups, n_short, _ = send_ref.shape
    for g in range(groups):
        send_ref[g] = query[:n_short]


def den_tile(den, width):
    shape = (den.shape[0], width)
    high = den.astype(BF16).astype(F32)
    low = den - high
    lane, row = lanes(shape), rows_of(shape) % SUB
    return jnp.where(lane == row, high, jnp.where(lane == row + SUB, low, 0.0))


def own_terms(rows, query, wk_ref, wv_ref, gain):
    new_key = head_unit(project(rows, wk_ref), gain).astype(BF16).astype(F32)
    new_value = project(rows, wv_ref).astype(BF16).astype(F32)
    own = [jnp.exp(c * math.sqrt(HEAD)) for c in head_cols(query * new_key)]
    rounded = [o.astype(BF16).astype(F32) for o in own]
    return spread_cols(own, query.shape), spread_cols(rounded, query.shape) * new_value


def cache_kernel(hit_ref, spread_ref, live_ref, q_ref, own_ref, rows_ref, wk_ref, wv_ref, gain_ref, lk_ref, lv_ref, k_ref, v_ref, out_ref, own_den_ref, own_num_ref, score_ref, num_ref, long_ref):
    own_den_ref[...], own_num_ref[...] = own_terms(
        rows_ref[...], own_ref[...].astype(F32), wk_ref, wv_ref, gain_ref[...]
    )
    slots, width, capacity = k_ref.shape
    groups, n_short, _ = q_ref.shape
    total = groups * n_short
    exp_rows = slots * SUB
    queries = q_ref[...].reshape(total, width)
    picked = jnp.dot(hit_ref[...], queries, preferred_element_type=F32)
    shape = (exp_rows, width)
    mask = (lanes(shape) // HEAD) == (rows_of(shape) % SUB)
    blocks = jnp.where(mask, picked * math.sqrt(HEAD), 0.0).astype(BF16)
    n_long = lk_ref.shape[0]
    long_query = own_ref[n_short : n_short + SUB].astype(F32) * math.sqrt(HEAD)
    mask8 = mask[:SUB]
    for s in range(0, slots, 2):
        keys = jnp.concatenate([k_ref[s], k_ref[s + 1]], 1)
        both = jnp.dot(blocks[s * SUB : (s + 2) * SUB], keys, preferred_element_type=F32)
        score_ref[s * SUB : (s + 1) * SUB] = both[:SUB, :capacity]
        score_ref[(s + 1) * SUB : (s + 2) * SUB] = both[SUB:, capacity:]
    weights = jnp.where(live_ref[...] > 0.0, jnp.exp(score_ref[...]), 0.0)
    tail = out_ref.shape[-1] - width
    real = rows_of((exp_rows, tail)) % SUB < width // HEAD
    dens = den_tile(jnp.sum(weights, -1, keepdims=True), tail)
    dens = jnp.where(real, dens, 0.0).astype(BF16)
    spread = spread_ref[...]
    top = rows_of((2 * SUB, capacity)) < SUB
    for s in range(0, slots, 2):
        at = slice(s * SUB, (s + 2) * SUB)
        pair = jnp.concatenate(
            [jnp.where(top, weights[at], 0.0), jnp.where(top, 0.0, weights[at])], 1
        )
        values = jnp.concatenate([v_ref[s], v_ref[s + 1]], 1)
        num_ref[at] = lax.dot_general(pair.astype(BF16), values, NT, preferred_element_type=F32)
    long_weights = []
    for i in range(n_long):
        row = jnp.broadcast_to(long_query[i : i + 1], mask8.shape)
        block = jnp.where(mask8, row, 0.0).astype(BF16)
        long_weights.append(jnp.exp(jnp.dot(block, lk_ref[i], preferred_element_type=F32)))
    long_ref[...] = jnp.zeros(long_ref.shape, F32)
    real8 = real[:SUB]
    for i in range(n_long):
        den = jnp.sum(long_weights[i], -1, keepdims=True)
        num = lax.dot_general(
            long_weights[i].astype(BF16), lv_ref[i], NT, preferred_element_type=F32
        )
        long_ref[i : i + 1, :width] = jnp.sum(jnp.where(mask8, num, 0.0), 0, keepdims=True)
        long_ref[i : i + 1, width:] = jnp.sum(
            jnp.where(real8, den_tile(den, tail), 0.0), 0, keepdims=True
        )
    extra = long_ref[...].astype(BF16)
    for g in range(groups):
        out_ref[g, n_short:, :] = extra
    num = jnp.where(mask, num_ref[...], 0.0).astype(BF16)
    sent = jnp.dot(spread, jnp.concatenate([num, dens], 1), preferred_element_type=F32)
    out_ref[:, :n_short, :] = sent.astype(BF16).reshape(groups, n_short, width + tail)


def combine_kernel(n_short, n_long, back_ref, den_ref, num_ref, w_ref, out_ref):
    width = num_ref.shape[-1]
    heads = width // HEAD
    total = back_ref[0].astype(F32)
    for g in range(1, back_ref.shape[0]):
        total = total + back_ref[g].astype(F32)
    dens = total[:, width:]
    cols = [dens[:, h : h + 1] + dens[:, SUB + h : SUB + h + 1] for h in range(heads)]
    den = den_ref[...] + spread_cols(cols, num_ref.shape)
    attended = ((total[:, :width] + num_ref[...]) / den).astype(BF16)
    proj = jnp.dot(attended, w_ref[...], preferred_element_type=F32)
    out_ref[...] = pack(proj, n_short, n_long).astype(BF16)


def pack(x, n_short, n_long):
    half, features = n_short // 2, x.shape[1]
    fold = half // n_long
    step = features // fold
    long_rows = x[n_short : n_short + n_long]
    folded = [long_rows[:, i * step : (i + 1) * step] for i in range(fold)]
    return jnp.concatenate([x[:half], x[half:n_short], jnp.concatenate(folded, 0)], 1)


def final_kernel(tp_ref, *refs):
    *part_refs, rows_ref, rate_ref, short_ref, long_ref = refs
    n_short, width = short_ref.shape
    n_long = long_ref.shape[0]
    features = rows_ref.shape[1]
    half = n_short // 2
    fold = half // n_long
    step = features // fold
    total = part_refs[0][...].astype(F32)
    for part in part_refs[1:]:
        total = total + part[...].astype(F32)
    short = jnp.concatenate([total[:, :features], total[:, features : 2 * features]], 0)
    folded = total[:, 2 * features :]
    long = jnp.concatenate([folded[i * n_long : (i + 1) * n_long] for i in range(fold)], 1)
    for proj, first, out_ref in ((short, 0, short_ref), (long, n_short, long_ref)):
        count = proj.shape[0]
        proj = proj * lax.rsqrt(jnp.sum(proj * proj, -1, keepdims=True) / features + EPS)
        state = rows_ref[...].astype(F32)[first : first + count]
        update = state + rate_ref[...] * (proj - state)
        square = jnp.sum(update * update, -1, keepdims=True)
        mine = update[:, :width]
        for t in range(1, features // width):
            mine = jnp.where(tp_ref[0] == t, update[:, t * width : (t + 1) * width], mine)
        out_ref[...] = (mine * lax.rsqrt(square / features + EPS)).astype(BF16)


def size_of(axis):
    return lax.axis_size(axis)


def from_all(x, axis):
    size = size_of(axis)
    got = []
    for k in range(size - 1, 0, -1):
        pairs = [(i, i ^ k if size & (size - 1) == 0 else (i + k) % size) for i in range(size)]
        got.append(lax.ppermute(x, axis, pairs))
    return [x, *got]


def exchange(x, axis):
    return lax.all_to_all(x, axis, split_axis=0, concat_axis=0, tiled=True)


VMEM = pl.BlockSpec(memory_space=pltpu.VMEM)
DISTANT = pl.BlockSpec(memory_space=pltpu.HBM)
SMEM = pl.BlockSpec(memory_space=pltpu.SMEM)


def call(kernel, outs, ins, flops, moved, scratch=(), scalars=0, limit=16, distant=0):
    return pl.pallas_call(
        kernel,
        out_shape=outs,
        in_specs=[SMEM] * scalars + [VMEM] * (len(ins) - scalars - distant) + [DISTANT] * distant,
        out_specs=jax.tree.map(lambda _: VMEM, outs),
        scratch_shapes=scratch,
        compiler_params=pltpu.CompilerParams(vmem_limit_bytes=limit * 1024 * 1024),
        cost_estimate=pl.CostEstimate(flops=flops, bytes_accessed=moved, transcendentals=0),
    )(*ins)


def on_device(
    short_hidden,
    long_hidden,
    short_len,
    short_slot,
    w_query,
    w_key,
    w_value,
    w_out,
    qk_gain,
    step_rate,
    short_keys,
    short_values,
    long_keys,
    long_values,
):
    n_short, width = short_hidden.shape
    n_long = long_hidden.shape[0]
    groups = size_of("seq")
    features = w_query.shape[0]
    slots, capacity, _ = short_keys.shape
    total = short_len.shape[0]
    pad = -(n_short + n_long) % SUB
    count = n_short + n_long + pad
    sent_width = -(-(width + 2 * SUB) // 128) * 128
    out = jax.ShapeDtypeStruct
    tp_index = lax.axis_index("tp").reshape(1)
    base = (lax.axis_index("seq") * slots).reshape(1)

    mine = call(
        join_kernel,
        out((count, width), BF16),
        tuple(pltpu.with_memory_space_constraint(a, pltpu.HBM) for a in (short_hidden, long_hidden)),
        0,
        4 * count * width,
        scratch=[
            pltpu.VMEM(short_hidden.shape, BF16),
            pltpu.VMEM(long_hidden.shape, BF16),
            pltpu.SemaphoreType.DMA((2,)),
        ],
        distant=2,
    )
    pieces = from_all(mine, "tp")
    w_query, w_key, w_value = w_query.T, w_key.T, w_value.T
    short_keys, short_values, long_keys, long_values = (
        jnp.swapaxes(a, 1, 2) for a in (short_keys, short_values, long_keys, long_values)
    )
    gain = call(gain_kernel, out((1, width), F32), (qk_gain.reshape(1, width),), 10**11, width)
    hit, spread, live, gain = call(
        prepare_kernel,
        (
            out((slots * SUB, total), BF16),
            out((total, slots * SUB), BF16),
            out((slots * SUB, capacity), F32),
            out((1, width), F32),
        ),
        (base, short_slot.reshape(1, total), short_len.reshape(1, total), gain),
        10**8,
        slots * SUB * total,
        scalars=1,
    )
    send, query, rows = call(
        query_kernel,
        (
            out((groups, n_short, width), BF16),
            out((count, width), BF16),
            out((count, features), BF16),
        ),
        (tp_index, *pieces, w_query, gain),
        10**11,
        6 * features * width,
        scratch=[pltpu.VMEM((len(pieces), count, width), F32)],
        scalars=1,
    )
    queries = exchange(send, "seq")
    sent, own_den, own_num = call(
        cache_kernel,
        (
            out((groups, count, sent_width), BF16),
            out((count, width), F32),
            out((count, width), F32),
        ),
        (hit, spread, live, queries, query, rows, w_key, w_value, gain, long_keys, long_values, short_keys, short_values),
        10**8,
        4 * short_keys.size + 4 * long_keys.size,
        scratch=[
            pltpu.VMEM((slots * SUB, capacity), F32),
            pltpu.VMEM((slots * SUB, width), F32),
            pltpu.VMEM((count - n_short, sent_width), F32),
        ],
    )
    back = exchange(sent, "seq")
    partial = call(
        functools.partial(combine_kernel, n_short, n_long),
        out((n_short // 2, 2 * features + 2 * n_long * features // n_short), BF16),
        (back, own_den, own_num, w_out),
        2 * count * features * width,
        2 * features * width,
    )
    partials = from_all(partial, "tp")
    return call(
        final_kernel,
        (out((n_short, width), BF16), out((n_long, width), BF16)),
        (tp_index, *partials, rows, step_rate.reshape(1, features)),
        10 * count * features,
        10 * count * features,
        scalars=1,
    )


def solution(mesh):
    return jax.shard_map(
        on_device,
        mesh=mesh,
        in_specs=(
            P("seq", "tp"),
            P(None, "tp"),
            P(),
            P(),
            P(None, "tp"),
            P(None, "tp"),
            P(None, "tp"),
            P("tp", None),
            P("tp"),
            P(),
            P("seq", None, "tp"),
            P("seq", None, "tp"),
            P(None, "seq", "tp"),
            P(None, "seq", "tp"),
        ),
        out_specs=(P("seq", "tp"), P(None, "tp")),
        check_vma=False,
    )
```
